256 devices in a mesh: row: 8 (over x, y_hi), col: 8 (over z), depth: 4 (over y_lo, core).
Axes of the slice: x: 4, y: 4 (y_hi: 2, y_lo: 2; y = y_hi * 2 + y_lo), z: 8, core: 2. Of those that a mesh axis runs over, the one named last changes fastest.
Arguments:
- context: bfloat16 [16384, 4096], P(('row', 'depth'), 'col'), may hold values from -6 to 6
- out_grad: bfloat16 [16384, 5120], P(('row', 'depth'), 'col'), may hold values from -6 to 6
- master: float32 [4096, 5120], P('row', 'col'), may hold values from -0.09375 to 0.09375
- first_moment: float32 [4096, 5120], P('row', 'col'), may hold values from -384 to 384
- second_moment: float32 [4096, 5120], P('row', 'col'), may hold values from 1638.4 to 163840
Outputs:
- input_grad: bfloat16 [16384, 4096], P(('row', 'depth'), 'col')
- new_master: float32 [4096, 5120], P('row', 'col')
- new_first: float32 [4096, 5120], P('row', 'col')
- new_second: float32 [4096, 5120], P('row', 'col')
The draws below stay inside these ranges and needn't reach their ends.
All inputs are finite; a program needn't handle non-finite values.
Results may differ from the reference program's by a relative error of at most 0.017.
Values may be sent and summed in bfloat16 or wider, within the bound.
A program may use at most 64 MiB of HBM per device.

```python
import math
import jax
import jax.numpy as jnp
from jax import lax

D = 5120
STEP = 10
H = 4096
TOKENS = 16384
N_COL = 8


def raised(result, key, source, target, blocks, factor):
    def block_of(dim):
        return (jnp.arange(result.shape[dim]) // (result.shape[dim] // blocks)).reshape((-1,) + (1,) * (result.ndim - 1 - dim))

    first = jax.random.permutation(key, blocks)[block_of(target)]
    far = (block_of(target) + blocks // 2) % blocks
    return jnp.where((block_of(source) == first) | (block_of(source) == far), factor * result, result)


def level_of(own_key, extent, split, low, top_value):
    factor_of, own = 1.0, jax.random.fold_in(own_key, 6)
    for position, parts in split:
        steps = jnp.exp(jax.random.uniform(jax.random.fold_in(own, position), (parts,), jnp.float32, low / len(split), top_value / len(split)))
        factor_of = factor_of * jnp.repeat(steps, extent[position] // parts).reshape([-1 if axis == position else 1 for axis in range(len(extent))])
    return factor_of


def normal_values(key, dims, spread, reach, split=(), dtype=jnp.bfloat16):
    level = level_of(key, dims, split, -0.22, 0.18) if split else 1.0
    drawn = jax.random.normal(key, dims, jnp.float32) * spread * level
    return jnp.minimum(jnp.maximum(drawn, -reach), reach).astype(dtype)


def bell_draw_with(own_key, shape, spread, limit, split, heavy, held_as=jnp.bfloat16):
    result = spread * jax.random.normal(own_key, shape, jnp.float32)
    if split:
        result = result * level_of(own_key, shape, split, -0.22, 0.18)
    return jnp.clip(raised(result, jax.random.fold_in(own_key, 3), *heavy), -limit, limit).astype(held_as)


def setup_inputs(seed: int = 0) -> dict:
    splits = jax.random.split(jax.random.key(seed), 6)
    context = bell_draw_with(splits[0], (TOKENS, H), 1.0, 6.0, ((0, 32), (1, 8)), (0, 1, 32, 2.75))
    out_grad = normal_values(splits[1], (TOKENS, D), 1.0, 6.0, ((0, 32), (1, 8)))
    master = normal_values(splits[2], (H, D), H ** -0.5, 0.09375, ((0, 8), (1, 8)), jnp.float32)
    first_moment = normal_values(splits[3], (H, D), (0.5 * TOKENS ** 0.5), 384.0, ((0, 8), (1, 8)), jnp.float32)
    second_moment = jnp.clip(jnp.exp(math.log(163840.0) - 4.6051702 * jax.random.uniform(splits[4], (H, D), jnp.float32) ** level_of(splits[4], (H, D), ((0, 8), (1, 8)), -0.2, 0.2)), 1638.4, 163840.0)
    return {"context": context, "out_grad": out_grad, "master": master, "first_moment": first_moment, "second_moment": second_moment}


beta_one = 0.9
beta_two = 0.95
adam_eps = 1e-08
learn_rate = 0.001
decay_rate = 0.1

def adam_update(gradient, master, first_moment, second_moment):
    new_first = beta_one * first_moment + (1.0 - beta_one) * gradient
    new_second = beta_two * second_moment + (1.0 - beta_two) * gradient * gradient
    first_hat = new_first / (1.0 - beta_one ** STEP)
    second_hat = new_second / (1.0 - beta_two ** STEP)
    new_master = master - learn_rate * (first_hat / (jnp.sqrt(second_hat) + adam_eps) + decay_rate * master)
    return (new_master, new_first, new_second)

def reference(context, out_grad, master, first_moment, second_moment):
    weight = master.astype(jnp.bfloat16)
    block_width = D // N_COL
    summed = jnp.zeros((TOKENS, H), jnp.float32)
    for column_block in range(N_COL):
        first_col = column_block * block_width
        partial_term = jnp.dot(out_grad[:, first_col:first_col + block_width], weight[:, first_col:first_col + block_width].T, preferred_element_type=jnp.float32)
        rounded = lax.optimization_barrier(partial_term.astype(jnp.bfloat16))
        summed = summed + rounded.astype(jnp.float32)
    input_grad = summed.astype(jnp.bfloat16)
    gradient = jnp.dot(context.T, out_grad, preferred_element_type=jnp.float32)
    new_master, new_first, new_second = adam_update(gradient, master, first_moment, second_moment)
    return (input_grad, new_master, new_first, new_second)
```

```python
import jax
import jax.numpy as jnp
from jax import lax
from jax.experimental import pallas as pl
from jax.experimental.pallas import tpu as pltpu
from jax.sharding import PartitionSpec as P

STEP = 10

beta_one = 0.9
beta_two = 0.95
adam_eps = 1e-08
learn_rate = 0.001
decay_rate = 0.1

MESH = pl.DeviceIdType.MESH
NZ = 8
U = 16


def adam_update(gradient, master, first_moment, second_moment):
    new_first = beta_one * first_moment + (1.0 - beta_one) * gradient
    new_second = beta_two * second_moment + (1.0 - beta_two) * gradient * gradient
    first_hat = new_first / (1.0 - beta_one**STEP)
    second_hat = new_second / (1.0 - beta_two**STEP)
    new_master = master - learn_rate * (
        first_hat / (jnp.sqrt(second_hat) + adam_eps) + decay_rate * master
    )
    return (new_master, new_first, new_second)


def mod(value, n):
    return lax.rem(value, jnp.int32(n))


def kernel(
    ctx_ref,
    og_ref,
    master_ref,
    ig_ref,
    grad_ref,
    og_all,
    ct_own,
    ct_sib,
    w16,
    w_in,
    w_pan,
    p_buf,
    r1,
    q_buf,
    r2,
    f_buf,
    gz,
    g_tile,
    g_sib,
    acc,
    ig_out,
    ig_in,
    z_send,
    z_recv,
    s_send,
    s_recv,
    m_send,
    m_recv,
    w_send,
    w_recv,
    r1_send,
    r1_recv,
    r2_send,
    r2_recv,
    h_send,
    h_recv,
    f_send,
    f_own_send,
    f_recv,
):
    row, z, dep = lax.axis_index("row"), lax.axis_index("col"), lax.axis_index("depth")
    x, yh = lax.div(row, jnp.int32(2)), mod(row, 2)
    yl, c = lax.div(dep, jnp.int32(2)), mod(dep, 2)
    y = yh * 2 + yl
    half = 16 * U
    tok = og_ref.shape[0]
    ht = tok // 2

    def z_peer(s):
        return (row, mod(z + s, NZ), dep)

    sibling = (row, z, yl * 2 + (1 - c))

    def x_peer(j):
        return (mod(x + j, 4) * 2 + yh, z, dep)

    def y_peer(j):
        yy = mod(y + j, 4)
        return (x * 2 + lax.div(yy, jnp.int32(2)), z, mod(yy, 2) * 2 + c)

    def remote(src, dst, send, recv, device):
        pltpu.make_async_remote_copy(
            src_ref=src,
            dst_ref=dst,
            send_sem=send,
            recv_sem=recv,
            device_id=device,
            device_id_type=MESH,
        ).start()

    def await_bytes(ref, sem):
        pltpu.make_async_copy(ref, ref, sem).wait()

    place = (
        pl.multiple_of(x * (4 * U) + y * U, U),
        pl.multiple_of(y * (4 * U) + x * U, U),
    )

    barrier = pltpu.get_barrier_semaphore()
    for s in range(1, NZ):
        pl.semaphore_signal(barrier, inc=1, device_id=z_peer(s), device_id_type=MESH)
    pl.semaphore_signal(barrier, inc=1, device_id=sibling, device_id_type=MESH)
    for j in range(8):
        for e in range(2):
            if j or e:
                pl.semaphore_signal(
                    barrier,
                    inc=1,
                    device_id=(mod(row + j, 8), z, mod(yl + e, 2) * 2 + c),
                    device_id_type=MESH,
                )
    w16[...] = master_ref[...].astype(jnp.bfloat16)
    ct_own[...] = ctx_ref[...].T
    pl.semaphore_wait(barrier, 23)

    def og(s, t):
        return og_ref if s == 0 and t == 0 else og_all.at[s, t]

    def part(ref, b):
        return ref.at[pl.ds(b * ht, ht)]

    def forward(s, b, d):
        if d == 0:
            to, peer = (s - 1) % NZ, z_peer(1)
        else:
            to, peer = (s + 1) % NZ, z_peer(NZ - 1)
        remote(
            part(og(s, 0), b), part(og_all.at[to, 0], b), z_send, z_recv.at[2 * to + b], peer
        )

    def to_sibling(s, b):
        remote(
            part(og(s, 0), b), part(og_all.at[s, 1], b), s_send, s_recv.at[s], sibling
        )

    def arrived(s, b):
        await_bytes(part(og_all.at[s, 0], b), z_recv.at[2 * s + b])

    forward(0, 0, 0)
    forward(0, 1, 1)
    forward(0, 1, 0)
    forward(0, 0, 1)

    ct_half = (1 - c) * half
    remote(
        ct_own.at[pl.ds(pl.multiple_of(ct_half, half), half)],
        ct_sib,
        m_send.at[0],
        m_recv.at[0],
        sibling,
    )
    to_sibling(0, 0)
    to_sibling(0, 1)

    odd = mod(z + row, 2)

    def w_place(row_to):
        xx, yy = lax.div(row_to, jnp.int32(2)), mod(row_to, 2) * 2 + yl
        a, b = xx + odd * (yy - xx), yy + odd * (xx - yy)
        return pl.ds(pl.multiple_of(c * half + a * (4 * U) + b * U, U), U)

    for j in range(1, 8):
        row_to = mod(row + j, 8)
        remote(
            w16.at[w_place(row_to)], w_in.at[row], w_send.at[0], w_recv.at[0], (row_to, z, dep)
        )
    w_in[row] = w16[w_place(row)]
    await_bytes(w_in.at[pl.ds(0, 7)], w_recv.at[0])

    for step in range(1, NZ):
        s = NZ - step
        remote(
            w_in.at[mod(z + step, NZ)],
            w_pan.at[s % 2, s // 2, pl.ds(place[s % 2], U)],
            w_send.at[1],
            w_recv.at[1],
            z_peer(step),
        )
    w_pan[0, 0, pl.ds(place[0], U)] = w_in[z]

    ct_mine = pl.ds(pl.multiple_of(c * half, half), half)

    def grad_partial(s):
        await_bytes(og_all.at[s, 1], s_recv.at[s])
        total = jnp.dot(ct_own[ct_mine, :], og(s, 0)[...], preferred_element_type=jnp.float32)
        total += jnp.dot(ct_sib[...], og_all[s, 1], preferred_element_type=jnp.float32)
        p_buf[s] = total.astype(jnp.bfloat16).reshape(4, 4 * U, total.shape[-1])
        axis, peer = (x, x_peer) if s % 2 == 0 else (y, y_peer)
        for j in range(1, 4):
            remote(
                p_buf.at[s, mod(axis + j, 4)],
                r1.at[s, j - 1],
                r1_send.at[s],
                r1_recv.at[s],
                peer(j),
            )

    def reduce_first(s):
        await_bytes(r1.at[s], r1_recv.at[s])
        axis = x if s % 2 == 0 else y
        total = p_buf[s, axis].astype(jnp.float32)
        for j in range(3):
            total += r1[s, j].astype(jnp.float32)
        q_buf[s] = total.astype(jnp.bfloat16).reshape(4, U, total.shape[-1])
        axis, peer = (y, y_peer) if s % 2 == 0 else (x, x_peer)
        for j in range(1, 4):
            remote(
                q_buf.at[s, mod(axis + j, 4)],
                r2.at[s, j - 1],
                r2_send.at[s],
                r2_recv.at[s],
                peer(j),
            )

    def reduce_second(s):
        await_bytes(r2.at[s], r2_recv.at[s])
        axis = y if s % 2 == 0 else x
        total = q_buf[s, axis].astype(jnp.float32)
        for j in range(3):
            total += r2[s, j].astype(jnp.float32)
        if s == 0:
            gz[0] = total.astype(jnp.bfloat16)
        else:
            f_buf[s] = total.astype(jnp.bfloat16)
            remote(f_buf.at[s], gz.at[s], h_send, h_recv.at[s], z_peer(s))

    def deliver(s):
        if s:
            await_bytes(gz.at[s], h_recv.at[s])
        row_to = mod(z + (NZ - s), NZ)
        spot = pl.ds(place[s % 2], U)
        remote(
            gz.at[s], g_tile.at[spot], f_send, f_recv, (row_to, z, (1 - yl) * 2 + c)
        )

        @pl.when(row_to != row)
        def _():
            remote(gz.at[s], g_tile.at[spot], f_own_send, f_recv, (row_to, z, dep))

        @pl.when(row_to == row)
        def _():
            g_tile[spot, :] = gz[s]

    def input_partial(s):
        w = w_pan[s % 2, s // 2]
        for t in range(2):
            term = lax.dot_general(
                og(s, t)[...], w, (((1,), (1,)), ((), ())), preferred_element_type=jnp.float32
            )
            if s == 0:
                acc[t] = term
            else:
                acc[t] += term

    await_bytes(ct_sib, m_recv.at[0])
    grad_partial(0)

    def w_gather(parity, axis_peer, rows, n, send, recv):
        view = w_pan.at[parity, :, rows]
        for j in range(1, 4):
            remote(view, view, send, recv, axis_peer(j))

    def w_gathered(parity, n, recv):
        await_bytes(w_pan.at[parity, :, pl.ds(0, 3 * n)], recv)

    await_bytes(w_in.at[pl.ds(0, 7)], w_recv.at[1])
    w_gather(0, y_peer, pl.ds(place[0], U), U, w_send.at[2], w_recv.at[2])
    w_gather(1, x_peer, pl.ds(place[1], U), U, w_send.at[3], w_recv.at[3])
    w_gathered(0, U, w_recv.at[2])
    w_gather(
        0, x_peer, pl.ds(pl.multiple_of(x * 4 * U, 4 * U), 4 * U), 4 * U, w_send.at[4], w_recv.at[4]
    )
    w_gathered(1, U, w_recv.at[3])
    w_gather(
        1, y_peer, pl.ds(pl.multiple_of(y * 4 * U, 4 * U), 4 * U), 4 * U, w_send.at[5], w_recv.at[5]
    )

    def pass_on(s_right, b_right, s_left, b_left, onward=True):
        arrived(s_right, b_right)
        if onward:
            forward(s_right, b_right, 0)
        to_sibling(s_right, b_right)
        arrived(s_left, b_left)
        if onward:
            forward(s_left, b_left, 1)
        to_sibling(s_left, b_left)

    pass_on(7, 0, 1, 1)
    reduce_first(0)
    w_gathered(0, 4 * U, w_recv.at[4])
    input_partial(0)
    reduce_second(0)
    deliver(0)
    w_gathered(1, 4 * U, w_recv.at[5])

    pass_on(7, 1, 1, 0)
    grad_partial(7)
    grad_partial(1)
    pass_on(6, 0, 2, 1)
    reduce_first(7)
    reduce_first(1)
    input_partial(7)
    reduce_second(7)
    reduce_second(1)
    pass_on(6, 1, 2, 0)
    grad_partial(6)
    grad_partial(2)
    deliver(7)
    deliver(1)
    pass_on(5, 0, 3, 1)
    reduce_first(6)
    reduce_first(2)
    input_partial(1)
    reduce_second(6)
    reduce_second(2)
    input_partial(6)
    pass_on(5, 1, 3, 0, onward=False)
    grad_partial(5)
    grad_partial(3)
    deliver(6)
    deliver(2)
    input_partial(2)
    reduce_first(5)
    reduce_first(3)
    input_partial(5)
    reduce_second(5)
    reduce_second(3)
    input_partial(3)
    deliver(5)
    deliver(3)
    arrived(4, 0)
    to_sibling(4, 0)
    arrived(4, 1)
    to_sibling(4, 1)
    grad_partial(4)
    input_partial(4)
    ig_out[...] = acc[1].astype(jnp.bfloat16)
    remote(ig_out, ig_in, m_send.at[1], m_recv.at[1], sibling)
    reduce_first(4)
    ig_ref[:, ct_mine] = acc[0].astype(jnp.bfloat16)
    reduce_second(4)
    await_bytes(ig_in, m_recv.at[1])
    ig_ref[:, pl.ds(pl.multiple_of(ct_half, half), half)] = ig_in[...]
    deliver(4)

    await_bytes(g_tile.at[pl.ds(0, 15 * U)], f_recv)
    remote(g_tile, g_sib, m_send.at[2], m_recv.at[2], sibling)
    grad_ref[ct_mine, :] = g_tile[...]
    await_bytes(g_sib, m_recv.at[2])
    grad_ref[pl.ds(pl.multiple_of(ct_half, half), half), :] = g_sib[...]

    await_bytes(og_all.at[pl.ds(0, 7), 0], z_send)
    await_bytes(og_all.at[:, 1], s_send)
    await_bytes(ct_sib, m_send.at[0])
    await_bytes(ig_in, m_send.at[1])
    await_bytes(g_sib, m_send.at[2])
    await_bytes(w_in.at[pl.ds(0, 7)], w_send.at[0])
    await_bytes(w_in.at[pl.ds(0, 7)], w_send.at[1])
    w_gathered(0, U, w_send.at[2])
    w_gathered(1, U, w_send.at[3])
    w_gathered(0, 4 * U, w_send.at[4])
    w_gathered(1, 4 * U, w_send.at[5])
    for s in range(NZ):
        await_bytes(r1.at[s], r1_send.at[s])
        await_bytes(r2.at[s], r2_send.at[s])
    await_bytes(f_buf.at[pl.ds(0, 7)], h_send)
    await_bytes(gz, f_send)
    await_bytes(gz.at[pl.ds(0, 7)], f_own_send)


def on_device(context, out_grad, master, first_moment, second_moment):
    tok, width = out_grad.shape
    bf16 = jnp.bfloat16
    half = 16 * U
    dma = pltpu.SemaphoreType.DMA
    vmem = pl.BlockSpec(memory_space=pltpu.VMEM)
    input_grad, gradient = pl.pallas_call(
        kernel,
        out_shape=(
            jax.ShapeDtypeStruct((tok, 2 * half), bf16),
            jax.ShapeDtypeStruct((2 * half, width), bf16),
        ),
        in_specs=[vmem] * 3,
        out_specs=(vmem, vmem),
        scratch_shapes=[
            pltpu.VMEM((NZ, 2, tok, width), bf16),
            pltpu.VMEM((2 * half, tok), bf16),
            pltpu.VMEM((half, tok), bf16),
            pltpu.VMEM((2 * half, width), bf16),
            pltpu.VMEM((8, U, width), bf16),
            pltpu.VMEM((2, NZ // 2, half, width), bf16),
            pltpu.VMEM((NZ, 4, 4 * U, width), bf16),
            pltpu.VMEM((NZ, 3, 4 * U, width), bf16),
            pltpu.VMEM((NZ, 4, U, width), bf16),
            pltpu.VMEM((NZ, 3, U, width), bf16),
            pltpu.VMEM((NZ, U, width), bf16),
            pltpu.VMEM((NZ, U, width), bf16),
            pltpu.VMEM((half, width), bf16),
            pltpu.VMEM((half, width), bf16),
            pltpu.VMEM((2, tok, half), jnp.float32),
            pltpu.VMEM((tok, half), bf16),
            pltpu.VMEM((tok, half), bf16),
            dma,
            dma((2 * NZ,)),
            dma,
            dma((NZ,)),
            dma((3,)),
            dma((3,)),
            dma((6,)),
            dma((6,)),
            dma((NZ,)),
            dma((NZ,)),
            dma((NZ,)),
            dma((NZ,)),
            dma,
            dma((NZ,)),
            dma,
            dma,
            dma,
        ],
        compiler_params=pltpu.CompilerParams(
            collective_id=0, has_side_effects=True, vmem_limit_bytes=50 * 1024 * 1024
        ),
        cost_estimate=pl.CostEstimate(
            flops=8 * tok * width * 2 * half * 2, bytes_accessed=4_000_000, transcendentals=0
        ),
    )(context, out_grad, master)
    new_master, new_first, new_second = adam_update(
        gradient.astype(jnp.float32), master, first_moment, second_moment
    )
    return (input_grad, new_master, new_first, new_second)


def solution(mesh):
    in_specs = (
        P(("row", "depth"), "col"),
        P(("row", "depth"), "col"),
        P("row", "col"),
        P("row", "col"),
        P("row", "col"),
    )
    out_specs = (P(("row", "depth"), "col"), P("row", "col"), P("row", "col"), P("row", "col"))
    return jax.shard_map(
        on_device, mesh=mesh, in_specs=in_specs, out_specs=out_specs, check_vma=False
    )
```

```python
import jax
import jax.numpy as jnp
from jax import lax
from jax.experimental import pallas as pl
from jax.experimental.pallas import tpu as pltpu
from jax.sharding import PartitionSpec as P

STEP = 10

beta_one = 0.9
beta_two = 0.95
adam_eps = 1e-08
learn_rate = 0.001
decay_rate = 0.1

MESH = pl.DeviceIdType.MESH
NZ = 8
U = 16


def adam_update(gradient, master, first_moment, second_moment):
    new_first = beta_one * first_moment + (1.0 - beta_one) * gradient
    new_second = beta_two * second_moment + (1.0 - beta_two) * gradient * gradient
    first_hat = new_first / (1.0 - beta_one**STEP)
    second_hat = new_second / (1.0 - beta_two**STEP)
    new_master = master - learn_rate * (
        first_hat / (jnp.sqrt(second_hat) + adam_eps) + decay_rate * master
    )
    return (new_master, new_first, new_second)


def mod(value, n):
    return lax.rem(value, jnp.int32(n))


def kernel(
    ctx_ref,
    og_ref,
    master_ref,
    ig_ref,
    grad_ref,
    ctx_v,
    master_v,
    og_all,
    ct_own,
    ct_sib,
    w16,
    w_in,
    w_pan,
    p_buf,
    r1,
    q_buf,
    r2,
    rd,
    f_buf,
    gz,
    g_tile,
    g_sib,
    acc,
    ig_out,
    ig_in,
    z_send,
    z_recv,
    s_send,
    s_recv,
    m_send,
    m_recv,
    w_send,
    w_recv,
    r1_send,
    r1_recv,
    r2_send,
    r2_recv,
    h_send,
    h_recv,
    f_send,
    f_own_send,
    f_recv,
    l_sem,
):
    row, z, dep = lax.axis_index("row"), lax.axis_index("col"), lax.axis_index("depth")
    x, yh = lax.div(row, jnp.int32(2)), mod(row, 2)
    yl, c = lax.div(dep, jnp.int32(2)), mod(dep, 2)
    y = yh * 2 + yl
    half = 16 * U
    tok = og_ref.shape[0]
    ht = tok // 2

    def z_peer(s):
        return (row, mod(z + s, NZ), dep)

    sibling = (row, z, yl * 2 + (1 - c))

    def x_peer(j):
        return (mod(x + j, 4) * 2 + yh, z, dep)

    def y_peer(j):
        yy = mod(y + j, 4)
        return (x * 2 + lax.div(yy, jnp.int32(2)), z, mod(yy, 2) * 2 + c)

    def remote(src, dst, send, recv, device):
        pltpu.make_async_remote_copy(
            src_ref=src,
            dst_ref=dst,
            send_sem=send,
            recv_sem=recv,
            device_id=device,
            device_id_type=MESH,
        ).start()

    def await_bytes(ref, sem):
        pltpu.make_async_copy(ref, ref, sem).wait()

    place = (
        pl.multiple_of(x * (4 * U) + y * U, U),
        pl.multiple_of(y * (4 * U) + x * U, U),
    )

    barrier = pltpu.get_barrier_semaphore()
    for s in range(1, NZ):
        pl.semaphore_signal(barrier, inc=1, device_id=z_peer(s), device_id_type=MESH)
    pl.semaphore_signal(barrier, inc=1, device_id=sibling, device_id_type=MESH)
    for j in range(8):
        for e in range(2):
            if j or e:
                pl.semaphore_signal(
                    barrier,
                    inc=1,
                    device_id=(mod(row + j, 8), z, mod(yl + e, 2) * 2 + c),
                    device_id_type=MESH,
                )
    pltpu.make_async_copy(master_ref, master_v, l_sem.at[0]).start()
    pltpu.make_async_copy(ctx_ref, ctx_v, l_sem.at[1]).start()
    pltpu.make_async_copy(og_ref, og_all.at[0, 0], l_sem.at[2]).start()
    await_bytes(master_v, l_sem.at[0])
    w16[...] = master_v[...].astype(jnp.bfloat16)
    await_bytes(ctx_v, l_sem.at[1])
    ct_own[...] = ctx_v[...].T
    pl.semaphore_wait(barrier, 23)

    def og(s, t):
        return og_all.at[s, t]

    def source(s):
        return og_ref if s == 0 else og_all.at[s, 0]

    def part(ref, b):
        return ref.at[pl.ds(b * ht, ht)]

    def forward(s, b, d):
        if d == 0:
            to, peer = (s - 1) % NZ, z_peer(1)
        else:
            to, peer = (s + 1) % NZ, z_peer(NZ - 1)
        remote(
            part(source(s), b), part(og_all.at[to, 0], b), z_send, z_recv.at[2 * to + b], peer
        )

    def to_sibling(s, b):
        remote(
            part(source(s), b), part(og_all.at[s, 1], b), s_send, s_recv.at[s], sibling
        )

    def arrived(s, b):
        await_bytes(part(og_all.at[s, 0], b), z_recv.at[2 * s + b])

    late = lax.div(mod(z + NZ - row, NZ), jnp.int32(4))

    def w_place(row_to):
        xx, yy = lax.div(row_to, jnp.int32(2)), mod(row_to, 2) * 2 + yl
        a, b = xx + late * (yy - xx), yy + late * (xx - yy)
        return pl.ds(pl.multiple_of(c * half + a * (4 * U) + b * U, U), U)

    for j in range(1, 8):
        row_to = mod(row + j, 8)
        remote(
            w16.at[w_place(row_to)], w_in.at[row], w_send.at[0], w_recv.at[0], (row_to, z, dep)
        )
    w_in[row] = w16[w_place(row)]
    forward(0, 0, 0)
    forward(0, 1, 1)
    ct_half = (1 - c) * half
    remote(
        ct_own.at[pl.ds(pl.multiple_of(ct_half, half), half)],
        ct_sib,
        m_send.at[0],
        m_recv.at[0],
        sibling,
    )

    to_sibling(0, 0)
    to_sibling(0, 1)

    await_bytes(w_in.at[pl.ds(0, 7)], w_recv.at[0])

    for step in range(1, NZ):
        s = NZ - step
        remote(
            w_in.at[mod(z + step, NZ)],
            w_pan.at[s // 4, s % 4, pl.ds(place[s // 4], U)],
            w_send.at[1],
            w_recv.at[1],
            z_peer(step),
        )
    w_pan[0, 0, pl.ds(place[0], U)] = w_in[z]

    ct_mine = pl.ds(pl.multiple_of(c * half, half), half)

    def grad_terms(s):
        total = jnp.dot(ct_own[ct_mine, :], og(s, 0)[...], preferred_element_type=jnp.float32)
        total += jnp.dot(ct_sib[...], og_all[s, 1], preferred_element_type=jnp.float32)
        return total.astype(jnp.bfloat16).reshape(4, 4 * U, total.shape[-1])

    def grad_partial(s):
        await_bytes(og_all.at[s, 1], s_recv.at[s])
        p_buf[s] = grad_terms(s)
        axis, peer = (x, x_peer) if s < 4 else (y, y_peer)
        for j in range(1, 4):
            remote(
                p_buf.at[s, mod(axis + j, 4)],
                r1.at[s, j - 1],
                r1_send.at[s],
                r1_recv.at[s],
                peer(j),
            )

    def reduce_first(s):
        await_bytes(r1.at[s], r1_recv.at[s])
        axis = x if s < 4 else y
        total = p_buf[s, axis].astype(jnp.float32)
        for j in range(3):
            total += r1[s, j].astype(jnp.float32)
        q_buf[s] = total.astype(jnp.bfloat16).reshape(4, U, total.shape[-1])
        axis, peer = (y, y_peer) if s < 4 else (x, x_peer)
        for j in range(1, 4):
            remote(
                q_buf.at[s, mod(axis + j, 4)],
                r2.at[s, j - 1],
                r2_send.at[s],
                r2_recv.at[s],
                peer(j),
            )

    def reduce_second(s):
        await_bytes(r2.at[s], r2_recv.at[s])
        axis = y if s < 4 else x
        total = q_buf[s, axis].astype(jnp.float32)
        for j in range(3):
            total += r2[s, j].astype(jnp.float32)
        if s == 0:
            gz[0] = total.astype(jnp.bfloat16)
        else:
            f_buf[s] = total.astype(jnp.bfloat16)
            remote(f_buf.at[s], gz.at[s], h_send, h_recv.at[s], z_peer(s))

    def grad_last():
        await_bytes(og_all.at[4, 1], s_recv.at[4])
        p_buf[4] = grad_terms(4)
        for jx in range(4):
            for jy in range(4):
                if jx or jy:
                    xx, yy = mod(x + jx, 4), mod(y + jy, 4)
                    remote(
                        p_buf.at[4, yy, pl.ds(pl.multiple_of(xx * U, U), U)],
                        rd.at[jx * 4 + jy - 1],
                        r1_send.at[4],
                        r1_recv.at[4],
                        (xx * 2 + lax.div(yy, jnp.int32(2)), z, mod(yy, 2) * 2 + c),
                    )

    def reduce_last():
        await_bytes(rd, r1_recv.at[4])
        total = p_buf[4, y, pl.ds(pl.multiple_of(x * U, U), U)].astype(jnp.float32)
        for j in range(15):
            total += rd[j].astype(jnp.float32)
        f_buf[4] = total.astype(jnp.bfloat16)
        remote(f_buf.at[4], gz.at[4], h_send, h_recv.at[4], z_peer(4))

    def deliver(s):
        if s:
            await_bytes(gz.at[s], h_recv.at[s])
        row_to = mod(z + (NZ - s), NZ)
        spot = pl.ds(place[s // 4], U)
        remote(
            gz.at[s], g_tile.at[spot], f_send, f_recv, (row_to, z, (1 - yl) * 2 + c)
        )

        @pl.when(row_to != row)
        def _():
            remote(gz.at[s], g_tile.at[spot], f_own_send, f_recv, (row_to, z, dep))

        @pl.when(row_to == row)
        def _():
            g_tile[spot, :] = gz[s]

    def input_partial(s):
        w = w_pan[s // 4, s % 4]
        for t in range(2):
            term = lax.dot_general(
                og(s, t)[...], w, (((1,), (1,)), ((), ())), preferred_element_type=jnp.float32
            )
            if s == 0:
                acc[t] = term
            else:
                acc[t] += term

    def w_gather(parity, axis_peer, rows, n, send, recv):
        view = w_pan.at[parity, :, rows]
        for j in range(1, 4):
            remote(view, view, send, recv, axis_peer(j))

    def w_gathered(parity, n, recv):
        await_bytes(w_pan.at[parity, :, pl.ds(0, 3 * n)], recv)

    def pass_on(s, b, d, onward=True):
        arrived(s, b)
        if onward:
            forward(s, b, d)
        to_sibling(s, b)

    rows_x = pl.ds(pl.multiple_of(x * 4 * U, 4 * U), 4 * U)
    rows_y = pl.ds(pl.multiple_of(y * 4 * U, 4 * U), 4 * U)

    await_bytes(w_in.at[pl.ds(0, 7)], w_recv.at[1])
    forward(0, 1, 0)
    forward(0, 0, 1)
    w_gather(0, y_peer, pl.ds(place[0], U), U, w_send.at[2], w_recv.at[2])
    w_gather(1, x_peer, pl.ds(place[1], U), U, w_send.at[3], w_recv.at[3])
    await_bytes(og_all.at[0, 0], l_sem.at[2])
    await_bytes(ct_sib, m_recv.at[0])
    pass_on(7, 0, 0)
    pass_on(1, 1, 1)
    grad_partial(0)
    w_gathered(0, U, w_recv.at[2])
    w_gather(0, x_peer, rows_x, 4 * U, w_send.at[4], w_recv.at[4])
    w_gathered(1, U, w_recv.at[3])
    w_gather(1, y_peer, rows_y, 4 * U, w_send.at[5], w_recv.at[5])
    pass_on(7, 1, 0)
    pass_on(1, 0, 1)
    grad_partial(7)
    grad_partial(1)
    reduce_first(0)
    pass_on(6, 0, 0)
    pass_on(2, 1, 1)
    pass_on(6, 1, 0)
    pass_on(2, 0, 1)
    reduce_first(7)
    reduce_first(1)
    grad_partial(6)
    grad_partial(2)
    reduce_second(0)
    reduce_second(7)
    reduce_second(1)
    pass_on(5, 0, 0)
    pass_on(3, 1, 1)
    pass_on(5, 1, 0, onward=False)
    pass_on(3, 0, 1, onward=False)
    reduce_first(6)
    reduce_first(2)
    grad_partial(5)
    grad_partial(3)
    deliver(0)
    deliver(7)
    deliver(1)
    w_gathered(0, 4 * U, w_recv.at[4])
    input_partial(0)
    input_partial(1)
    w_gathered(1, 4 * U, w_recv.at[5])
    input_partial(7)
    reduce_second(6)
    reduce_second(2)
    pass_on(4, 0, 0, onward=False)
    pass_on(4, 1, 1, onward=False)
    reduce_first(5)
    reduce_first(3)
    grad_last()
    deliver(6)
    deliver(2)
    reduce_second(5)
    reduce_second(3)
    input_partial(2)
    input_partial(6)
    input_partial(5)
    input_partial(3)
    reduce_last()
    deliver(5)
    deliver(3)
    input_partial(4)
    ig_out[...] = acc[1].astype(jnp.bfloat16)
    remote(ig_out, ig_in, m_send.at[1], m_recv.at[1], sibling)
    deliver(4)
    ig_ref[:, ct_mine] = acc[0].astype(jnp.bfloat16)
    ct_other = pl.ds(pl.multiple_of(ct_half, half), half)

    await_bytes(g_tile.at[pl.ds(0, 15 * U)], f_recv)
    remote(g_tile, g_sib, m_send.at[2], m_recv.at[2], sibling)
    grad_ref[ct_mine, :] = g_tile[...]
    await_bytes(ig_in, m_recv.at[1])
    ig_ref[:, ct_other] = ig_in[...]
    await_bytes(g_sib, m_recv.at[2])
    grad_ref[ct_other, :] = g_sib[...]

    await_bytes(og_all.at[pl.ds(0, 7), 0], z_send)
    await_bytes(og_all.at[:, 1], s_send)
    await_bytes(ct_sib, m_send.at[0])
    await_bytes(ig_in, m_send.at[1])
    await_bytes(g_sib, m_send.at[2])
    await_bytes(w_in.at[pl.ds(0, 7)], w_send.at[0])
    await_bytes(w_in.at[pl.ds(0, 7)], w_send.at[1])
    w_gathered(0, U, w_send.at[2])
    w_gathered(1, U, w_send.at[3])
    w_gathered(0, 4 * U, w_send.at[4])
    w_gathered(1, 4 * U, w_send.at[5])
    for s in range(NZ):
        if s == 4:
            await_bytes(rd, r1_send.at[s])
        else:
            await_bytes(r1.at[s], r1_send.at[s])
            await_bytes(r2.at[s], r2_send.at[s])
    await_bytes(f_buf.at[pl.ds(0, 7)], h_send)
    await_bytes(gz, f_send)
    await_bytes(gz.at[pl.ds(0, 7)], f_own_send)


def on_device(context, out_grad, master, first_moment, second_moment):
    tok, width = out_grad.shape
    bf16 = jnp.bfloat16
    half = 16 * U
    dma = pltpu.SemaphoreType.DMA
    vmem = pl.BlockSpec(memory_space=pltpu.VMEM)
    input_grad, gradient = pl.pallas_call(
        kernel,
        out_shape=(
            jax.ShapeDtypeStruct((tok, 2 * half), bf16),
            jax.ShapeDtypeStruct((2 * half, width), bf16),
        ),
        in_specs=[pl.BlockSpec(memory_space=pltpu.HBM)] * 3,
        out_specs=(vmem, vmem),
        scratch_shapes=[
            pltpu.VMEM((tok, 2 * half), bf16),
            pltpu.VMEM((2 * half, width), jnp.float32),
            pltpu.VMEM((NZ, 2, tok, width), bf16),
            pltpu.VMEM((2 * half, tok), bf16),
            pltpu.VMEM((half, tok), bf16),
            pltpu.VMEM((2 * half, width), bf16),
            pltpu.VMEM((8, U, width), bf16),
            pltpu.VMEM((2, NZ // 2, half, width), bf16),
            pltpu.VMEM((NZ, 4, 4 * U, width), bf16),
            pltpu.VMEM((NZ, 3, 4 * U, width), bf16),
            pltpu.VMEM((NZ, 4, U, width), bf16),
            pltpu.VMEM((NZ, 3, U, width), bf16),
            pltpu.VMEM((15, U, width), bf16),
            pltpu.VMEM((NZ, U, width), bf16),
            pltpu.VMEM((NZ, U, width), bf16),
            pltpu.VMEM((half, width), bf16),
            pltpu.VMEM((half, width), bf16),
            pltpu.VMEM((2, tok, half), jnp.float32),
            pltpu.VMEM((tok, half), bf16),
            pltpu.VMEM((tok, half), bf16),
            dma,
            dma((2 * NZ,)),
            dma,
            dma((NZ,)),
            dma((3,)),
            dma((3,)),
            dma((6,)),
            dma((6,)),
            dma((NZ,)),
            dma((NZ,)),
            dma((NZ,)),
            dma((NZ,)),
            dma,
            dma((NZ,)),
            dma,
            dma,
            dma,
            dma((3,)),
        ],
        compiler_params=pltpu.CompilerParams(
            collective_id=0, has_side_effects=True, vmem_limit_bytes=60 * 1024 * 1024
        ),
        cost_estimate=pl.CostEstimate(
            flops=8 * tok * width * 2 * half * 2, bytes_accessed=4_000_000, transcendentals=0
        ),
    )(context, out_grad, master)
    new_master, new_first, new_second = adam_update(
        gradient.astype(jnp.float32), master, first_moment, second_moment
    )
    return (input_grad, new_master, new_first, new_second)


def solution(mesh):
    in_specs = (
        P(("row", "depth"), "col"),
        P(("row", "depth"), "col"),
        P("row", "col"),
        P("row", "col"),
        P("row", "col"),
    )
    out_specs = (P(("row", "depth"), "col"), P("row", "col"), P("row", "col"), P("row", "col"))
    return jax.shard_map(
        on_device, mesh=mesh, in_specs=in_specs, out_specs=out_specs, check_vma=False
    )
```

```python
import jax
import jax.numpy as jnp
from jax import lax
from jax.experimental import pallas as pl
from jax.experimental.pallas import tpu as pltpu
from jax.sharding import PartitionSpec as P

STEP = 10

beta_one = 0.9
beta_two = 0.95
adam_eps = 1e-08
learn_rate = 0.001
decay_rate = 0.1

MESH = pl.DeviceIdType.MESH
NZ = 8
CUT = 256
U = 16


def adam_update(gradient, master, first_moment, second_moment):
    new_first = beta_one * first_moment + (1.0 - beta_one) * gradient
    new_second = beta_two * second_moment + (1.0 - beta_two) * gradient * gradient
    first_hat = new_first * (1.0 / (1.0 - beta_one**STEP))
    second_hat = new_second * (1.0 / (1.0 - beta_two**STEP))
    new_master = master - learn_rate * (
        first_hat / (jnp.sqrt(second_hat) + adam_eps) + decay_rate * master
    )
    return (new_master, new_first, new_second)


def mod(value, n):
    return lax.rem(value, jnp.int32(n))


def kernel(
    ctx_ref,
    og_ref,
    master_ref,
    ig_ref,
    grad_ref,
    ctx_v,
    master_v,
    og_all,
    ct_own,
    ct_sib,
    w16,
    w_in,
    w_pan,
    p_buf,
    r1,
    q_buf,
    r2,
    rd,
    f_buf,
    gz,
    g_tile,
    g_sib,
    acc,
    ig_out,
    ig_in,
    z_send,
    z_recv,
    s_send,
    s_recv,
    m_send,
    m_recv,
    w_send,
    w_recv,
    r1_send,
    r1_recv,
    r2_send,
    r2_recv,
    h_send,
    h_recv,
    f_send,
    f_own_send,
    f_recv,
    l_sem,
):
    row, z, dep = lax.axis_index("row"), lax.axis_index("col"), lax.axis_index("depth")
    x, yh = lax.div(row, jnp.int32(2)), mod(row, 2)
    yl, c = lax.div(dep, jnp.int32(2)), mod(dep, 2)
    y = yh * 2 + yl
    half = 16 * U
    tok = og_ref.shape[0]
    ht = tok // 2

    def z_peer(s):
        return (row, mod(z + s, NZ), dep)

    sibling = (row, z, yl * 2 + (1 - c))

    def x_peer(j):
        return (mod(x + j, 4) * 2 + yh, z, dep)

    def y_peer(j):
        yy = mod(y + j, 4)
        return (x * 2 + lax.div(yy, jnp.int32(2)), z, mod(yy, 2) * 2 + c)

    def remote(src, dst, send, recv, device):
        pltpu.make_async_remote_copy(
            src_ref=src,
            dst_ref=dst,
            send_sem=send,
            recv_sem=recv,
            device_id=device,
            device_id_type=MESH,
        ).start()

    def await_bytes(ref, sem):
        pltpu.make_async_copy(ref, ref, sem).wait()

    place = (
        pl.multiple_of(x * (4 * U) + y * U, U),
        pl.multiple_of(y * (4 * U) + x * U, U),
    )

    barrier = pltpu.get_barrier_semaphore()
    for s in range(1, NZ):
        pl.semaphore_signal(barrier, inc=1, device_id=z_peer(s), device_id_type=MESH)
    pl.semaphore_signal(barrier, inc=1, device_id=sibling, device_id_type=MESH)
    for j in range(8):
        for e in range(2):
            if j or e:
                pl.semaphore_signal(
                    barrier,
                    inc=1,
                    device_id=(mod(row + j, 8), z, mod(yl + e, 2) * 2 + c),
                    device_id_type=MESH,
                )
    pltpu.make_async_copy(master_ref, master_v, l_sem.at[0]).start()
    pltpu.make_async_copy(ctx_ref, ctx_v, l_sem.at[1]).start()
    pltpu.make_async_copy(og_ref, og_all.at[0, 0], l_sem.at[2]).start()
    pl.semaphore_wait(barrier, 23)

    def og(s, t):
        return og_all.at[s, t]

    def source(s):
        return og_ref if s == 0 else og_all.at[s, 0]

    cols = (pl.ds(0, CUT), pl.ds(CUT, og_ref.shape[1] - CUT))

    def part(ref, b, d=None):
        return ref.at[:, cols[b]] if d is None else ref.at[pl.ds(d * ht, ht), cols[b]]

    def token_half(s, d):
        return d if s == 4 else None

    def forward(s, b, d):
        to, peer = ((s - 1) % NZ, z_peer(1)) if d == 0 else (s + 1, z_peer(NZ - 1))
        h = token_half(to, d)
        remote(
            part(source(s), b, h),
            part(og_all.at[to, 0], b, h),
            z_send,
            z_recv.at[d, to, b],
            peer,
        )

    def to_sibling(s, b, d=0):
        h = token_half(s, d)
        remote(
            part(source(s), b, h), part(og_all.at[s, 1], b, h), s_send, s_recv.at[s, b], sibling
        )

    def arrived(s, b, d):
        await_bytes(part(og_all.at[s, 0], b, token_half(s, d)), z_recv.at[d, s, b])

    forward(0, 0, 0)
    forward(0, 0, 1)
    await_bytes(master_v, l_sem.at[0])
    w16[...] = master_v[...].astype(jnp.bfloat16)

    late = lax.div(mod(z + NZ - row, NZ), jnp.int32(4))

    def w_place(row_to):
        xx, yy = lax.div(row_to, jnp.int32(2)), mod(row_to, 2) * 2 + yl
        a, b = xx + late * (yy - xx), yy + late * (xx - yy)
        return pl.ds(pl.multiple_of(c * half + a * (4 * U) + b * U, U), U)

    for j in range(1, 8):
        row_to = mod(row + j, 8)
        remote(
            w16.at[w_place(row_to)], w_in.at[row], w_send.at[0], w_recv.at[0], (row_to, z, dep)
        )
    w_in[row] = w16[w_place(row)]
    await_bytes(ctx_v, l_sem.at[1])
    ct_own[...] = ctx_v[...].T
    ct_half = (1 - c) * half
    remote(
        ct_own.at[pl.ds(pl.multiple_of(ct_half, half), half)],
        ct_sib,
        m_send.at[0],
        m_recv.at[0],
        sibling,
    )

    to_sibling(0, 0)
    to_sibling(0, 1)

    await_bytes(w_in.at[pl.ds(0, 7)], w_recv.at[0])

    for step in range(1, NZ):
        s = NZ - step
        remote(
            w_in.at[mod(z + step, NZ)],
            w_pan.at[s // 4, s % 4, pl.ds(place[s // 4], U)],
            w_send.at[1],
            w_recv.at[1],
            z_peer(step),
        )
    w_pan[0, 0, pl.ds(place[0], U)] = w_in[z]

    ct_mine = pl.ds(pl.multiple_of(c * half, half), half)

    def grad_terms(s, b):
        await_bytes(part(og_all.at[s, 1], b), s_recv.at[s, b])
        total = jnp.dot(
            ct_own[ct_mine, :], og_all[s, 0, :, cols[b]], preferred_element_type=jnp.float32
        )
        total += jnp.dot(
            ct_sib[...], og_all[s, 1, :, cols[b]], preferred_element_type=jnp.float32
        )
        p_buf[s, :, :, cols[b]] = total.astype(jnp.bfloat16).reshape(4, 4 * U, total.shape[-1])

    def grad_partial(s, b):
        grad_terms(s, b)
        axis, peer = (x, x_peer) if s < 4 else (y, y_peer)
        for j in range(1, 4):
            remote(
                p_buf.at[s, mod(axis + j, 4), :, cols[b]],
                r1.at[s, j - 1, :, cols[b]],
                r1_send.at[s],
                r1_recv.at[s],
                peer(j),
            )

    def reduce_first(s):
        await_bytes(r1.at[s], r1_recv.at[s])
        axis = x if s < 4 else y
        total = p_buf[s, axis].astype(jnp.float32)
        for j in range(3):
            total += r1[s, j].astype(jnp.float32)
        q_buf[s] = total.astype(jnp.bfloat16).reshape(4, U, total.shape[-1])
        axis, peer = (y, y_peer) if s < 4 else (x, x_peer)
        for j in range(1, 4):
            remote(
                q_buf.at[s, mod(axis + j, 4)],
                r2.at[s, j - 1],
                r2_send.at[s],
                r2_recv.at[s],
                peer(j),
            )

    def reduce_second(s):
        await_bytes(r2.at[s], r2_recv.at[s])
        axis = y if s < 4 else x
        total = q_buf[s, axis].astype(jnp.float32)
        for j in range(3):
            total += r2[s, j].astype(jnp.float32)
        if s == 0:
            gz[0] = total.astype(jnp.bfloat16)
        else:
            f_buf[s] = total.astype(jnp.bfloat16)
            remote(f_buf.at[s], gz.at[s], h_send, h_recv.at[s], z_peer(s))

    def grad_last(b):
        grad_terms(4, b)
        for jx in range(4):
            for jy in range(4):
                if jx or jy:
                    xx, yy = mod(x + jx, 4), mod(y + jy, 4)
                    remote(
                        p_buf.at[4, yy, pl.ds(pl.multiple_of(xx * U, U), U), cols[b]],
                        rd.at[jx * 4 + jy - 1, :, cols[b]],
                        r1_send.at[4],
                        r1_recv.at[4],
                        (xx * 2 + lax.div(yy, jnp.int32(2)), z, mod(yy, 2) * 2 + c),
                    )

    def reduce_last():
        await_bytes(rd, r1_recv.at[4])
        total = p_buf[4, y, pl.ds(pl.multiple_of(x * U, U), U)].astype(jnp.float32)
        for j in range(15):
            total += rd[j].astype(jnp.float32)
        f_buf[4] = total.astype(jnp.bfloat16)
        remote(f_buf.at[4], gz.at[4], h_send, h_recv.at[4], z_peer(4))

    def deliver(s):
        if s:
            await_bytes(gz.at[s], h_recv.at[s])
        row_to = mod(z + (NZ - s), NZ)
        spot = pl.ds(place[s // 4], U)
        remote(
            gz.at[s], g_tile.at[spot], f_send, f_recv, (row_to, z, (1 - yl) * 2 + c)
        )

        @pl.when(row_to != row)
        def _():
            remote(gz.at[s], g_tile.at[spot], f_own_send, f_recv, (row_to, z, dep))

        @pl.when(row_to == row)
        def _():
            g_tile[spot, :] = gz[s]

    def input_partial(s):
        w = w_pan[s // 4, s % 4]
        for t in range(2):
            term = lax.dot_general(
                og(s, t)[...], w, (((1,), (1,)), ((), ())), preferred_element_type=jnp.float32
            )
            if s == 0:
                acc[t] = term
            else:
                acc[t] += term

    def w_gather(parity, axis_peer, rows, n, send, recv):
        view = w_pan.at[parity, :, rows]
        for j in range(1, 4):
            remote(view, view, send, recv, axis_peer(j))

    def w_gathered(parity, n, recv):
        await_bytes(w_pan.at[parity, :, pl.ds(0, 3 * n)], recv)

    def pass_on(s, b, d):
        arrived(s, b, d)
        if s != 4:
            forward(s, b, d)
        to_sibling(s, b, d)

    rows_x = pl.ds(pl.multiple_of(x * 4 * U, 4 * U), 4 * U)
    rows_y = pl.ds(pl.multiple_of(y * 4 * U, 4 * U), 4 * U)

    forward(0, 1, 0)
    forward(0, 1, 1)
    await_bytes(og_all.at[0, 0], l_sem.at[2])
    await_bytes(ct_sib, m_recv.at[0])
    grad_partial(0, 0)
    grad_partial(0, 1)
    pass_on(7, 0, 0)
    pass_on(1, 0, 1)
    await_bytes(w_in.at[pl.ds(0, 7)], w_recv.at[1])
    w_gather(0, y_peer, pl.ds(place[0], U), U, w_send.at[2], w_recv.at[2])
    w_gather(1, x_peer, pl.ds(place[1], U), U, w_send.at[3], w_recv.at[3])
    grad_partial(7, 0)
    grad_partial(1, 0)
    pass_on(7, 1, 0)
    pass_on(1, 1, 1)
    w_gathered(0, U, w_recv.at[2])
    w_gather(0, x_peer, rows_x, 4 * U, w_send.at[4], w_recv.at[4])
    w_gathered(1, U, w_recv.at[3])
    w_gather(1, y_peer, rows_y, 4 * U, w_send.at[5], w_recv.at[5])
    grad_partial(7, 1)
    grad_partial(1, 1)
    reduce_first(0)
    pass_on(6, 0, 0)
    pass_on(2, 0, 1)
    grad_partial(6, 0)
    grad_partial(2, 0)
    pass_on(6, 1, 0)
    pass_on(2, 1, 1)
    reduce_first(7)
    reduce_first(1)
    grad_partial(6, 1)
    grad_partial(2, 1)
    pass_on(5, 0, 0)
    pass_on(3, 0, 1)
    reduce_second(0)
    reduce_second(7)
    reduce_second(1)
    grad_partial(5, 0)
    grad_partial(3, 0)
    reduce_first(6)
    reduce_first(2)
    deliver(0)
    pass_on(5, 1, 0)
    pass_on(3, 1, 1)
    grad_partial(5, 1)
    grad_partial(3, 1)
    reduce_second(6)
    reduce_second(2)
    w_gathered(0, 4 * U, w_recv.at[4])
    input_partial(0)
    pass_on(4, 0, 0)
    pass_on(4, 0, 1)
    input_partial(1)
    deliver(7)
    deliver(1)
    input_partial(2)
    grad_last(0)
    pass_on(4, 1, 0)
    pass_on(4, 1, 1)
    reduce_first(5)
    reduce_first(3)
    grad_last(1)
    w_gathered(1, 4 * U, w_recv.at[5])
    input_partial(7)
    input_partial(6)
    reduce_second(5)
    reduce_second(3)
    input_partial(5)
    input_partial(3)
    reduce_last()
    deliver(6)
    deliver(2)
    input_partial(4)
    ig_out[...] = acc[1].astype(jnp.bfloat16)
    remote(ig_out, ig_in, m_send.at[1], m_recv.at[1], sibling)
    deliver(5)
    deliver(3)
    deliver(4)
    ig_ref[:, ct_mine] = acc[0].astype(jnp.bfloat16)
    ct_other = pl.ds(pl.multiple_of(ct_half, half), half)

    await_bytes(g_tile.at[pl.ds(0, 15 * U)], f_recv)
    remote(g_tile, g_sib, m_send.at[2], m_recv.at[2], sibling)
    grad_ref[ct_mine, :] = g_tile[...]
    await_bytes(ig_in, m_recv.at[1])
    ig_ref[:, ct_other] = ig_in[...]
    await_bytes(g_sib, m_recv.at[2])
    grad_ref[ct_other, :] = g_sib[...]

    await_bytes(og_all.at[pl.ds(0, 7), 0], z_send)
    await_bytes(og_all.at[:, 1], s_send)
    await_bytes(ct_sib, m_send.at[0])
    await_bytes(ig_in, m_send.at[1])
    await_bytes(g_sib, m_send.at[2])
    await_bytes(w_in.at[pl.ds(0, 7)], w_send.at[0])
    await_bytes(w_in.at[pl.ds(0, 7)], w_send.at[1])
    w_gathered(0, U, w_send.at[2])
    w_gathered(1, U, w_send.at[3])
    w_gathered(0, 4 * U, w_send.at[4])
    w_gathered(1, 4 * U, w_send.at[5])
    for s in range(NZ):
        if s == 4:
            await_bytes(rd, r1_send.at[s])
        else:
            await_bytes(r1.at[s], r1_send.at[s])
            await_bytes(r2.at[s], r2_send.at[s])
    await_bytes(f_buf.at[pl.ds(0, 7)], h_send)
    await_bytes(gz, f_send)
    await_bytes(gz.at[pl.ds(0, 7)], f_own_send)


def on_device(context, out_grad, master, first_moment, second_moment):
    tok, width = out_grad.shape
    bf16 = jnp.bfloat16
    half = 16 * U
    dma = pltpu.SemaphoreType.DMA
    vmem = pl.BlockSpec(memory_space=pltpu.VMEM)
    input_grad, gradient = pl.pallas_call(
        kernel,
        out_shape=(
            pltpu.VMEM((tok, 2 * half), bf16),
            pltpu.VMEM((2 * half, width), bf16),
        ),
        in_specs=[pl.BlockSpec(memory_space=pltpu.HBM)] * 3,
        out_specs=(vmem, vmem),
        scratch_shapes=[
            pltpu.VMEM((tok, 2 * half), bf16),
            pltpu.VMEM((2 * half, width), jnp.float32),
            pltpu.VMEM((NZ, 2, tok, width), bf16),
            pltpu.VMEM((2 * half, tok), bf16),
            pltpu.VMEM((half, tok), bf16),
            pltpu.VMEM((2 * half, width), bf16),
            pltpu.VMEM((8, U, width), bf16),
            pltpu.VMEM((2, NZ // 2, half, width), bf16),
            pltpu.VMEM((NZ, 4, 4 * U, width), bf16),
            pltpu.VMEM((NZ, 3, 4 * U, width), bf16),
            pltpu.VMEM((NZ, 4, U, width), bf16),
            pltpu.VMEM((NZ, 3, U, width), bf16),
            pltpu.VMEM((15, U, width), bf16),
            pltpu.VMEM((NZ, U, width), bf16),
            pltpu.VMEM((NZ, U, width), bf16),
            pltpu.VMEM((half, width), bf16),
            pltpu.VMEM((half, width), bf16),
            pltpu.VMEM((2, tok, half), jnp.float32),
            pltpu.VMEM((tok, half), bf16),
            pltpu.VMEM((tok, half), bf16),
            dma,
            dma((2, NZ, 2)),
            dma,
            dma((NZ, 2)),
            dma((3,)),
            dma((3,)),
            dma((6,)),
            dma((6,)),
            dma((NZ,)),
            dma((NZ,)),
            dma((NZ,)),
            dma((NZ,)),
            dma,
            dma((NZ,)),
            dma,
            dma,
            dma,
            dma((3,)),
        ],
        compiler_params=pltpu.CompilerParams(
            collective_id=0, has_side_effects=True, vmem_limit_bytes=56 * 1024 * 1024
        ),
        cost_estimate=pl.CostEstimate(
            flops=8 * tok * width * 2 * half * 2, bytes_accessed=4_000_000, transcendentals=0
        ),
    )(context, out_grad, master)
    new_master, new_first, new_second = adam_update(
        gradient.astype(jnp.float32), master, first_moment, second_moment
    )
    return (input_grad, new_master, new_first, new_second)


def solution(mesh):
    in_specs = (
        P(("row", "depth"), "col"),
        P(("row", "depth"), "col"),
        P("row", "col"),
        P("row", "col"),
        P("row", "col"),
    )
    out_specs = (P(("row", "depth"), "col"), P("row", "col"), P("row", "col"), P("row", "col"))
    return jax.shard_map(
        on_device, mesh=mesh, in_specs=in_specs, out_specs=out_specs, check_vma=False
    )
```

```python
import jax
import jax.numpy as jnp
from jax import lax
from jax.experimental import pallas as pl
from jax.experimental.pallas import tpu as pltpu
from jax.sharding import PartitionSpec as P

STEP = 10

beta_one = 0.9
beta_two = 0.95
adam_eps = 1e-08
learn_rate = 0.001
decay_rate = 0.1

MESH = pl.DeviceIdType.MESH
NZ = 8
PIECES = 4
CUT = 256
U = 16


def adam_update(gradient, master, first_moment, second_moment):
    new_first = beta_one * first_moment + (1.0 - beta_one) * gradient
    new_second = beta_two * second_moment + (1.0 - beta_two) * gradient * gradient
    first_hat = new_first * (1.0 / (1.0 - beta_one**STEP))
    second_hat = new_second * (1.0 / (1.0 - beta_two**STEP))
    new_master = master - learn_rate * (
        first_hat / (jnp.sqrt(second_hat) + adam_eps) + decay_rate * master
    )
    return (new_master, new_first, new_second)


def mod(value, n):
    return lax.rem(value, jnp.int32(n))


def kernel(
    ctx_ref,
    og_ref,
    master_ref,
    ig_ref,
    grad_ref,
    ctx_v,
    master_v,
    og_all,
    ct_own,
    ct_sib,
    w16,
    w_in,
    w_pan,
    p_buf,
    r1,
    q_buf,
    r2,
    rd,
    f_buf,
    gz,
    g_tile,
    g_sib,
    acc,
    ig_out,
    ig_in,
    z_send,
    z_recv,
    s_send,
    s_recv,
    m_send,
    m_recv,
    w_send,
    w_recv,
    r1_send,
    r1_recv,
    r2_send,
    r2_recv,
    h_send,
    h_recv,
    f_send,
    f_own_send,
    f_recv,
    l_sem,
):
    row, z, dep = lax.axis_index("row"), lax.axis_index("col"), lax.axis_index("depth")
    x, yh = lax.div(row, jnp.int32(2)), mod(row, 2)
    yl, c = lax.div(dep, jnp.int32(2)), mod(dep, 2)
    y = yh * 2 + yl
    half = 16 * U
    tok = og_ref.shape[0]
    ht = tok // 2

    def z_peer(s):
        return (row, mod(z + s, NZ), dep)

    sibling = (row, z, yl * 2 + (1 - c))

    def x_peer(j):
        return (mod(x + j, 4) * 2 + yh, z, dep)

    def y_peer(j):
        yy = mod(y + j, 4)
        return (x * 2 + lax.div(yy, jnp.int32(2)), z, mod(yy, 2) * 2 + c)

    def remote(src, dst, send, recv, device):
        pltpu.make_async_remote_copy(
            src_ref=src,
            dst_ref=dst,
            send_sem=send,
            recv_sem=recv,
            device_id=device,
            device_id_type=MESH,
        ).start()

    def await_bytes(ref, sem):
        pltpu.make_async_copy(ref, ref, sem).wait()

    place = (
        pl.multiple_of(x * (4 * U) + y * U, U),
        pl.multiple_of(y * (4 * U) + x * U, U),
    )

    barrier = pltpu.get_barrier_semaphore()
    for s in range(1, NZ):
        pl.semaphore_signal(barrier, inc=1, device_id=z_peer(s), device_id_type=MESH)
    pl.semaphore_signal(barrier, inc=1, device_id=sibling, device_id_type=MESH)
    for j in range(8):
        for e in range(2):
            if j or e:
                pl.semaphore_signal(
                    barrier,
                    inc=1,
                    device_id=(mod(row + j, 8), z, mod(yl + e, 2) * 2 + c),
                    device_id_type=MESH,
                )
    pltpu.make_async_copy(master_ref, master_v, l_sem.at[0]).start()
    pltpu.make_async_copy(ctx_ref, ctx_v, l_sem.at[1]).start()
    pltpu.make_async_copy(og_ref, og_all.at[0, 0], l_sem.at[2]).start()
    pl.semaphore_wait(barrier, 23)

    def og(s, t):
        return og_all.at[s, t]

    def source(s):
        return og_ref if s == 0 else og_all.at[s, 0]

    cols = (pl.ds(0, CUT), pl.ds(CUT, og_ref.shape[1] - CUT))

    def part(ref, b, d=None):
        return ref.at[:, cols[b]] if d is None else ref.at[pl.ds(d * ht, ht), cols[b]]

    def token_half(s, d):
        return d if s == 4 else None

    def forward(s, b, d):
        to, peer = ((s - 1) % NZ, z_peer(1)) if d == 0 else (s + 1, z_peer(NZ - 1))
        h = token_half(to, d)
        remote(
            part(source(s), b, h),
            part(og_all.at[to, 0], b, h),
            z_send,
            z_recv.at[d, to, b],
            peer,
        )

    def to_sibling(s, b, d=0):
        h = token_half(s, d)
        remote(
            part(source(s), b, h), part(og_all.at[s, 1], b, h), s_send, s_recv.at[s, b], sibling
        )

    def arrived(s, b, d):
        await_bytes(part(og_all.at[s, 0], b, token_half(s, d)), z_recv.at[d, s, b])

    forward(0, 0, 0)
    forward(0, 0, 1)
    await_bytes(master_v, l_sem.at[0])
    w16[...] = master_v[...].astype(jnp.bfloat16)

    late = lax.div(mod(z + NZ - row, NZ), jnp.int32(4))

    def w_place(row_to):
        xx, yy = lax.div(row_to, jnp.int32(2)), mod(row_to, 2) * 2 + yl
        a, b = xx + late * (yy - xx), yy + late * (xx - yy)
        return pl.ds(pl.multiple_of(c * half + a * (4 * U) + b * U, U), U)

    for j in range(1, 8):
        row_to = mod(row + j, 8)
        remote(
            w16.at[w_place(row_to)], w_in.at[row], w_send.at[0], w_recv.at[0], (row_to, z, dep)
        )
    w_in[row] = w16[w_place(row)]
    await_bytes(ctx_v, l_sem.at[1])
    ct_own[...] = ctx_v[...].T
    ct_half = (1 - c) * half
    remote(
        ct_own.at[pl.ds(pl.multiple_of(ct_half, half), half)],
        ct_sib,
        m_send.at[0],
        m_recv.at[0],
        sibling,
    )

    to_sibling(0, 0)
    to_sibling(0, 1)

    await_bytes(w_in.at[pl.ds(0, 7)], w_recv.at[0])

    for step in range(1, NZ):
        s = NZ - step
        remote(
            w_in.at[mod(z + step, NZ)],
            w_pan.at[s // 4, s % 4, pl.ds(place[s // 4], U)],
            w_send.at[1],
            w_recv.at[1],
            z_peer(step),
        )
    w_pan[0, 0, pl.ds(place[0], U)] = w_in[z]

    ct_mine = pl.ds(pl.multiple_of(c * half, half), half)

    def grad_terms(s, b):
        await_bytes(part(og_all.at[s, 1], b), s_recv.at[s, b])
        total = jnp.dot(
            ct_own[ct_mine, :], og_all[s, 0, :, cols[b]], preferred_element_type=jnp.float32
        )
        total += jnp.dot(
            ct_sib[...], og_all[s, 1, :, cols[b]], preferred_element_type=jnp.float32
        )
        p_buf[s, :, :, cols[b]] = total.astype(jnp.bfloat16).reshape(4, 4 * U, total.shape[-1])

    def grad_partial(s, b):
        grad_terms(s, b)
        axis, peer = (x, x_peer) if s < 4 else (y, y_peer)
        for j in range(1, 4):
            remote(
                p_buf.at[s, mod(axis + j, 4), :, cols[b]],
                r1.at[s, j - 1, :, cols[b]],
                r1_send.at[s],
                r1_recv.at[s],
                peer(j),
            )

    def reduce_first(s):
        await_bytes(r1.at[s], r1_recv.at[s])
        axis = x if s < 4 else y
        total = p_buf[s, axis].astype(jnp.float32)
        for j in range(3):
            total += r1[s, j].astype(jnp.float32)
        q_buf[s] = total.astype(jnp.bfloat16).reshape(4, U, total.shape[-1])
        axis, peer = (y, y_peer) if s < 4 else (x, x_peer)
        for j in range(1, 4):
            remote(
                q_buf.at[s, mod(axis + j, 4)],
                r2.at[s, j - 1],
                r2_send.at[s],
                r2_recv.at[s],
                peer(j),
            )

    def reduce_second(s):
        await_bytes(r2.at[s], r2_recv.at[s])
        axis = y if s < 4 else x
        total = q_buf[s, axis].astype(jnp.float32)
        for j in range(3):
            total += r2[s, j].astype(jnp.float32)
        if s == 0:
            gz[0] = total.astype(jnp.bfloat16)
        else:
            f_buf[s] = total.astype(jnp.bfloat16)
            remote(f_buf.at[s], gz.at[s], h_send, h_recv.at[s], z_peer(s))

    def grad_last(b):
        grad_terms(4, b)
        for jx in range(4):
            for jy in range(4):
                if jx or jy:
                    xx, yy = mod(x + jx, 4), mod(y + jy, 4)
                    remote(
                        p_buf.at[4, yy, pl.ds(pl.multiple_of(xx * U, U), U), cols[b]],
                        rd.at[jx * 4 + jy - 1, :, cols[b]],
                        r1_send.at[4],
                        r1_recv.at[4],
                        (xx * 2 + lax.div(yy, jnp.int32(2)), z, mod(yy, 2) * 2 + c),
                    )

    def reduce_last():
        await_bytes(rd, r1_recv.at[4])
        total = p_buf[4, y, pl.ds(pl.multiple_of(x * U, U), U)].astype(jnp.float32)
        for j in range(15):
            total += rd[j].astype(jnp.float32)
        f_buf[4] = total.astype(jnp.bfloat16)
        remote(f_buf.at[4], gz.at[4], h_send, h_recv.at[4], z_peer(4))

    def deliver(s):
        if s:
            await_bytes(gz.at[s], h_recv.at[s])
        row_to = mod(z + (NZ - s), NZ)
        spot = pl.ds(place[s // 4], U)
        remote(
            gz.at[s], g_tile.at[spot], f_send, f_recv, (row_to, z, (1 - yl) * 2 + c)
        )

        @pl.when(row_to != row)
        def _():
            remote(gz.at[s], g_tile.at[spot], f_own_send, f_recv, (row_to, z, dep))

        @pl.when(row_to == row)
        def _():
            g_tile[spot, :] = gz[s]

    def input_partial(s):
        w = w_pan[s // 4, s % 4]
        for t in range(2):
            term = lax.dot_general(
                og(s, t)[...], w, (((1,), (1,)), ((), ())), preferred_element_type=jnp.float32
            )
            if s == 0:
                acc[t] = term
            else:
                acc[t] += term

    def w_gather(parity, axis_peer, rows, n, send, recv):
        view = w_pan.at[parity, :, rows]
        for j in range(1, 4):
            remote(view, view, send, recv, axis_peer(j))

    def w_gathered(parity, n, recv):
        await_bytes(w_pan.at[parity, :, pl.ds(0, 3 * n)], recv)

    def pass_on(s, b, d):
        arrived(s, b, d)
        if s != 4:
            forward(s, b, d)
        to_sibling(s, b, d)

    rows_x = pl.ds(pl.multiple_of(x * 4 * U, 4 * U), 4 * U)
    rows_y = pl.ds(pl.multiple_of(y * 4 * U, 4 * U), 4 * U)

    forward(0, 1, 0)
    forward(0, 1, 1)
    await_bytes(og_all.at[0, 0], l_sem.at[2])
    await_bytes(ct_sib, m_recv.at[0])
    grad_partial(0, 0)
    grad_partial(0, 1)
    pass_on(7, 0, 0)
    pass_on(1, 0, 1)
    await_bytes(w_in.at[pl.ds(0, 7)], w_recv.at[1])
    w_gather(0, y_peer, pl.ds(place[0], U), U, w_send.at[2], w_recv.at[2])
    w_gather(1, x_peer, pl.ds(place[1], U), U, w_send.at[3], w_recv.at[3])
    grad_partial(7, 0)
    grad_partial(1, 0)
    pass_on(7, 1, 0)
    pass_on(1, 1, 1)
    w_gathered(0, U, w_recv.at[2])
    w_gather(0, x_peer, rows_x, 4 * U, w_send.at[4], w_recv.at[4])
    w_gathered(1, U, w_recv.at[3])
    w_gather(1, y_peer, rows_y, 4 * U, w_send.at[5], w_recv.at[5])
    grad_partial(7, 1)
    grad_partial(1, 1)
    reduce_first(0)
    pass_on(6, 0, 0)
    pass_on(2, 0, 1)
    grad_partial(6, 0)
    grad_partial(2, 0)
    pass_on(6, 1, 0)
    pass_on(2, 1, 1)
    reduce_first(7)
    reduce_first(1)
    grad_partial(6, 1)
    grad_partial(2, 1)
    pass_on(5, 0, 0)
    pass_on(3, 0, 1)
    reduce_second(0)
    reduce_second(7)
    reduce_second(1)
    grad_partial(5, 0)
    grad_partial(3, 0)
    reduce_first(6)
    reduce_first(2)
    deliver(0)
    pass_on(5, 1, 0)
    pass_on(3, 1, 1)
    grad_partial(5, 1)
    grad_partial(3, 1)
    reduce_second(6)
    reduce_second(2)
    w_gathered(0, 4 * U, w_recv.at[4])
    input_partial(0)
    pass_on(4, 0, 0)
    pass_on(4, 0, 1)
    input_partial(1)
    input_partial(2)
    grad_last(0)
    pass_on(4, 1, 0)
    pass_on(4, 1, 1)
    reduce_first(5)
    reduce_first(3)
    grad_last(1)
    w_gathered(1, 4 * U, w_recv.at[5])
    input_partial(7)
    input_partial(6)
    reduce_second(5)
    reduce_second(3)
    input_partial(5)
    input_partial(3)
    reduce_last()
    deliver(7)
    deliver(1)
    deliver(6)
    deliver(2)
    input_partial(4)
    ig_out[...] = acc[1].astype(jnp.bfloat16)
    remote(ig_out, ig_in, m_send.at[1], m_recv.at[1], sibling)
    deliver(5)
    deliver(3)
    deliver(4)
    ig_ref[:, ct_mine] = acc[0].astype(jnp.bfloat16)
    ct_other = pl.ds(pl.multiple_of(ct_half, half), half)

    await_bytes(g_tile.at[pl.ds(0, 15 * U)], f_recv)
    remote(g_tile, g_sib, m_send.at[2], m_recv.at[2], sibling)
    grad_ref[ct_mine, :] = g_tile[...]
    await_bytes(ig_in, m_recv.at[1])
    ig_ref[:, ct_other] = ig_in[...]
    await_bytes(g_sib, m_recv.at[2])
    grad_ref[ct_other, :] = g_sib[...]

    await_bytes(og_all.at[pl.ds(0, 7), 0], z_send)
    await_bytes(og_all.at[:, 1], s_send)
    await_bytes(ct_sib, m_send.at[0])
    await_bytes(ig_in, m_send.at[1])
    await_bytes(g_sib, m_send.at[2])
    await_bytes(w_in.at[pl.ds(0, 7)], w_send.at[0])
    await_bytes(w_in.at[pl.ds(0, 7)], w_send.at[1])
    w_gathered(0, U, w_send.at[2])
    w_gathered(1, U, w_send.at[3])
    w_gathered(0, 4 * U, w_send.at[4])
    w_gathered(1, 4 * U, w_send.at[5])
    for s in range(NZ):
        if s == 4:
            await_bytes(rd, r1_send.at[s])
        else:
            await_bytes(r1.at[s], r1_send.at[s])
            await_bytes(r2.at[s], r2_send.at[s])
    await_bytes(f_buf.at[pl.ds(0, 7)], h_send)
    await_bytes(gz, f_send)
    await_bytes(gz.at[pl.ds(0, 7)], f_own_send)


def update_kernel(
    input_ref,
    grad_ref,
    master_ref,
    first_ref,
    second_ref,
    input_out,
    master_out,
    first_out,
    second_out,
    master_v,
    first_v,
    second_v,
    input_sem,
    out_sem,
):
    copies = [pltpu.make_async_copy(input_ref, input_out, input_sem)]
    copies[0].start()
    n = grad_ref.shape[0] // PIECES
    for i in range(PIECES):
        rows = pl.ds(i * n, n)
        results = adam_update(
            grad_ref[rows, :].astype(jnp.float32),
            master_ref[rows, :],
            first_ref[rows, :],
            second_ref[rows, :],
        )
        held = (master_v, first_v, second_v)
        outs = (master_out, first_out, second_out)
        for k in range(3):
            held[k][rows, :] = results[k]
            copy = pltpu.make_async_copy(held[k].at[rows], outs[k].at[rows], out_sem.at[i, k])
            copy.start()
            copies.append(copy)
    for copy in copies:
        copy.wait()


def on_device(context, out_grad, master, first_moment, second_moment):
    tok, width = out_grad.shape
    bf16 = jnp.bfloat16
    half = 16 * U
    dma = pltpu.SemaphoreType.DMA
    vmem = pl.BlockSpec(memory_space=pltpu.VMEM)
    input_grad, gradient = pl.pallas_call(
        kernel,
        out_shape=(
            pltpu.VMEM((tok, 2 * half), bf16),
            pltpu.VMEM((2 * half, width), bf16),
        ),
        in_specs=[pl.BlockSpec(memory_space=pltpu.HBM)] * 3,
        out_specs=(vmem, vmem),
        scratch_shapes=[
            pltpu.VMEM((tok, 2 * half), bf16),
            pltpu.VMEM((2 * half, width), jnp.float32),
            pltpu.VMEM((NZ, 2, tok, width), bf16),
            pltpu.VMEM((2 * half, tok), bf16),
            pltpu.VMEM((half, tok), bf16),
            pltpu.VMEM((2 * half, width), bf16),
            pltpu.VMEM((8, U, width), bf16),
            pltpu.VMEM((2, NZ // 2, half, width), bf16),
            pltpu.VMEM((NZ, 4, 4 * U, width), bf16),
            pltpu.VMEM((NZ, 3, 4 * U, width), bf16),
            pltpu.VMEM((NZ, 4, U, width), bf16),
            pltpu.VMEM((NZ, 3, U, width), bf16),
            pltpu.VMEM((15, U, width), bf16),
            pltpu.VMEM((NZ, U, width), bf16),
            pltpu.VMEM((NZ, U, width), bf16),
            pltpu.VMEM((half, width), bf16),
            pltpu.VMEM((half, width), bf16),
            pltpu.VMEM((2, tok, half), jnp.float32),
            pltpu.VMEM((tok, half), bf16),
            pltpu.VMEM((tok, half), bf16),
            dma,
            dma((2, NZ, 2)),
            dma,
            dma((NZ, 2)),
            dma((3,)),
            dma((3,)),
            dma((6,)),
            dma((6,)),
            dma((NZ,)),
            dma((NZ,)),
            dma((NZ,)),
            dma((NZ,)),
            dma,
            dma((NZ,)),
            dma,
            dma,
            dma,
            dma((3,)),
        ],
        compiler_params=pltpu.CompilerParams(
            collective_id=0, has_side_effects=True, vmem_limit_bytes=56 * 1024 * 1024
        ),
        cost_estimate=pl.CostEstimate(
            flops=8 * tok * width * 2 * half * 2, bytes_accessed=4_000_000, transcendentals=0
        ),
    )(context, out_grad, master)
    hbm = pl.BlockSpec(memory_space=pltpu.HBM)
    tile = jax.ShapeDtypeStruct(master.shape, jnp.float32)
    return pl.pallas_call(
        update_kernel,
        out_shape=(jax.ShapeDtypeStruct(input_grad.shape, bf16), tile, tile, tile),
        in_specs=[vmem] * 5,
        out_specs=(hbm,) * 4,
        scratch_shapes=[
            pltpu.VMEM(master.shape, jnp.float32),
            pltpu.VMEM(master.shape, jnp.float32),
            pltpu.VMEM(master.shape, jnp.float32),
            dma,
            dma((PIECES, 3)),
        ],
        compiler_params=pltpu.CompilerParams(vmem_limit_bytes=8 * 1024 * 1024),
        cost_estimate=pl.CostEstimate(
            flops=20 * master.size, bytes_accessed=12 * master.size, transcendentals=2 * master.size
        ),
    )(input_grad, gradient, master, first_moment, second_moment)


def solution(mesh):
    in_specs = (
        P(("row", "depth"), "col"),
        P(("row", "depth"), "col"),
        P("row", "col"),
        P("row", "col"),
        P("row", "col"),
    )
    out_specs = (P(("row", "depth"), "col"), P("row", "col"), P("row", "col"), P("row", "col"))
    return jax.shard_map(
        on_device, mesh=mesh, in_specs=in_specs, out_specs=out_specs, check_vma=False
    )
```

```python
import jax
import jax.numpy as jnp
from jax import lax
from jax.experimental import pallas as pl
from jax.experimental.pallas import tpu as pltpu
from jax.sharding import PartitionSpec as P

STEP = 10

beta_one = 0.9
beta_two = 0.95
adam_eps = 1e-08
learn_rate = 0.001
decay_rate = 0.1

MESH = pl.DeviceIdType.MESH
NZ = 8
PIECES = 4
CUT = 256
U = 16


def adam_update(gradient, master, first_moment, second_moment):
    new_first = beta_one * first_moment + (1.0 - beta_one) * gradient
    new_second = beta_two * second_moment + (1.0 - beta_two) * gradient * gradient
    first_hat = new_first * (1.0 / (1.0 - beta_one**STEP))
    second_hat = new_second * (1.0 / (1.0 - beta_two**STEP))
    new_master = master - learn_rate * (
        first_hat / (jnp.sqrt(second_hat) + adam_eps) + decay_rate * master
    )
    return (new_master, new_first, new_second)


def mod(value, n):
    return lax.rem(value, jnp.int32(n))


def kernel(
    ctx_ref,
    og_ref,
    master_ref,
    ig_ref,
    grad_ref,
    ctx_v,
    master_v,
    og_all,
    ct_own,
    ct_sib,
    w16,
    w_in,
    w_pan,
    p_buf,
    r1,
    q_buf,
    r2,
    rd,
    f_buf,
    gz,
    g_tile,
    g_sib,
    acc,
    ig_out,
    ig_in,
    z_send,
    z_recv,
    s_send,
    s_recv,
    m_send,
    m_recv,
    w_send,
    w_recv,
    r1_send,
    r1_recv,
    r2_send,
    r2_recv,
    h_send,
    h_recv,
    f_send,
    f_own_send,
    f_recv,
    l_sem,
    d_recv,
    h_last_recv,
):
    row, z, dep = lax.axis_index("row"), lax.axis_index("col"), lax.axis_index("depth")
    x, yh = lax.div(row, jnp.int32(2)), mod(row, 2)
    yl, c = lax.div(dep, jnp.int32(2)), mod(dep, 2)
    y = yh * 2 + yl
    half = 16 * U
    tok = og_ref.shape[0]
    ht = tok // 2

    def z_peer(s):
        return (row, mod(z + s, NZ), dep)

    sibling = (row, z, yl * 2 + (1 - c))

    def x_peer(j):
        return (mod(x + j, 4) * 2 + yh, z, dep)

    def y_peer(j):
        yy = mod(y + j, 4)
        return (x * 2 + lax.div(yy, jnp.int32(2)), z, mod(yy, 2) * 2 + c)

    def remote(src, dst, send, recv, device):
        pltpu.make_async_remote_copy(
            src_ref=src,
            dst_ref=dst,
            send_sem=send,
            recv_sem=recv,
            device_id=device,
            device_id_type=MESH,
        ).start()

    def await_bytes(ref, sem):
        pltpu.make_async_copy(ref, ref, sem).wait()

    place = (
        pl.multiple_of(x * (4 * U) + y * U, U),
        pl.multiple_of(y * (4 * U) + x * U, U),
    )

    pltpu.make_async_copy(master_ref, master_v, l_sem.at[0]).start()
    pltpu.make_async_copy(ctx_ref, ctx_v, l_sem.at[1]).start()
    pltpu.make_async_copy(og_ref, og_all.at[0, 0], l_sem.at[2]).start()
    barrier = pltpu.get_barrier_semaphore()
    for s in range(1, NZ):
        pl.semaphore_signal(barrier, inc=1, device_id=z_peer(s), device_id_type=MESH)
    pl.semaphore_signal(barrier, inc=1, device_id=sibling, device_id_type=MESH)
    for j in range(8):
        for e in range(2):
            if j or e:
                pl.semaphore_signal(
                    barrier,
                    inc=1,
                    device_id=(mod(row + j, 8), z, mod(yl + e, 2) * 2 + c),
                    device_id_type=MESH,
                )
    pl.semaphore_wait(barrier, 23)

    def og(s, t):
        return og_all.at[s, t]

    def source(s):
        return og_ref if s == 0 else og_all.at[s, 0]

    cols = (pl.ds(0, CUT), pl.ds(CUT, og_ref.shape[1] - CUT))

    def part(ref, b, d=None):
        return ref.at[:, cols[b]] if d is None else ref.at[pl.ds(d * ht, ht), cols[b]]

    def token_half(s, d):
        return d if s == 4 else None

    def forward(s, b, d):
        to, peer = ((s - 1) % NZ, z_peer(1)) if d == 0 else (s + 1, z_peer(NZ - 1))
        h = token_half(to, d)
        remote(
            part(source(s), b, h),
            part(og_all.at[to, 0], b, h),
            z_send,
            z_recv.at[d, to, b],
            peer,
        )

    def to_sibling(s, b, d=0):
        h = token_half(s, d)
        remote(
            part(source(s), b, h), part(og_all.at[s, 1], b, h), s_send, s_recv.at[s, b], sibling
        )

    def arrived(s, b, d):
        await_bytes(part(og_all.at[s, 0], b, token_half(s, d)), z_recv.at[d, s, b])

    forward(0, 0, 0)
    forward(0, 0, 1)
    await_bytes(master_v, l_sem.at[0])
    w16[...] = master_v[...].astype(jnp.bfloat16)

    late = lax.div(mod(z + NZ - row, NZ), jnp.int32(4))

    def w_place(row_to):
        xx, yy = lax.div(row_to, jnp.int32(2)), mod(row_to, 2) * 2 + yl
        a, b = xx + late * (yy - xx), yy + late * (xx - yy)
        return pl.ds(pl.multiple_of(c * half + a * (4 * U) + b * U, U), U)

    for j in range(1, 8):
        row_to = mod(row + j, 8)
        remote(
            w16.at[w_place(row_to)], w_in.at[row], w_send.at[0], w_recv.at[0], (row_to, z, dep)
        )
    w_in[row] = w16[w_place(row)]
    await_bytes(ctx_v, l_sem.at[1])
    ct_own[...] = ctx_v[...].T
    ct_half = (1 - c) * half
    remote(
        ct_own.at[pl.ds(pl.multiple_of(ct_half, half), half)],
        ct_sib,
        m_send.at[0],
        m_recv.at[0],
        sibling,
    )

    to_sibling(0, 0)
    to_sibling(0, 1)

    await_bytes(w_in.at[pl.ds(0, 7)], w_recv.at[0])

    for step in range(1, NZ):
        s = NZ - step
        remote(
            w_in.at[mod(z + step, NZ)],
            w_pan.at[s // 4, s % 4, pl.ds(place[s // 4], U)],
            w_send.at[1],
            w_recv.at[1],
            z_peer(step),
        )
    w_pan[0, 0, pl.ds(place[0], U)] = w_in[z]

    ct_mine = pl.ds(pl.multiple_of(c * half, half), half)

    def grad_terms(s, b):
        await_bytes(part(og_all.at[s, 1], b), s_recv.at[s, b])
        total = jnp.dot(
            ct_own[ct_mine, :], og_all[s, 0, :, cols[b]], preferred_element_type=jnp.float32
        )
        total += jnp.dot(
            ct_sib[...], og_all[s, 1, :, cols[b]], preferred_element_type=jnp.float32
        )
        p_buf[s, :, :, cols[b]] = total.astype(jnp.bfloat16).reshape(4, 4 * U, total.shape[-1])

    def grad_partial(s, b):
        grad_terms(s, b)
        axis, peer = (x, x_peer) if s < 4 else (y, y_peer)
        for j in range(1, 4):
            remote(
                p_buf.at[s, mod(axis + j, 4), :, cols[b]],
                r1.at[s, j - 1, :, cols[b]],
                r1_send.at[s],
                r1_recv.at[s],
                peer(j),
            )

    def reduce_first(s):
        await_bytes(r1.at[s], r1_recv.at[s])
        axis = x if s < 4 else y
        total = p_buf[s, axis].astype(jnp.float32)
        for j in range(3):
            total += r1[s, j].astype(jnp.float32)
        q_buf[s] = total.astype(jnp.bfloat16).reshape(4, U, total.shape[-1])
        axis, peer = (y, y_peer) if s < 4 else (x, x_peer)
        for j in range(1, 4):
            remote(
                q_buf.at[s, mod(axis + j, 4)],
                r2.at[s, j - 1],
                r2_send.at[s],
                r2_recv.at[s],
                peer(j),
            )

    def reduce_second(s):
        await_bytes(r2.at[s], r2_recv.at[s])
        axis = y if s < 4 else x
        total = q_buf[s, axis].astype(jnp.float32)
        for j in range(3):
            total += r2[s, j].astype(jnp.float32)
        if s == 0:
            gz[0] = total.astype(jnp.bfloat16)
        else:
            f_buf[s] = total.astype(jnp.bfloat16)
            remote(f_buf.at[s], gz.at[s], h_send, h_recv.at[s], z_peer(s))

    def grad_last(b):
        grad_terms(4, b)
        for jx in range(4):
            for jy in range(4):
                if jx or jy:
                    xx, yy = mod(x + jx, 4), mod(y + jy, 4)
                    remote(
                        p_buf.at[4, yy, pl.ds(pl.multiple_of(xx * U, U), U), cols[b]],
                        rd.at[jx * 4 + jy - 1, :, cols[b]],
                        r1_send.at[4],
                        d_recv.at[b],
                        (xx * 2 + lax.div(yy, jnp.int32(2)), z, mod(yy, 2) * 2 + c),
                    )

    def reduce_last(b):
        await_bytes(rd.at[:, :, cols[b]], d_recv.at[b])
        total = p_buf[4, y, pl.ds(pl.multiple_of(x * U, U), U), cols[b]].astype(jnp.float32)
        for j in range(15):
            total += rd[j, :, cols[b]].astype(jnp.float32)
        f_buf[4, :, cols[b]] = total.astype(jnp.bfloat16)
        remote(
            f_buf.at[4, :, cols[b]], gz.at[4, :, cols[b]], h_send, h_last_recv.at[b], z_peer(4)
        )

    def deliver(s, b=None):
        span = slice(None) if b is None else cols[b]
        if s == 4:
            await_bytes(gz.at[4, :, span], h_last_recv.at[b])
        elif s:
            await_bytes(gz.at[s], h_recv.at[s])
        row_to = mod(z + (NZ - s), NZ)
        spot = pl.ds(place[s // 4], U)
        source_piece, target = gz.at[s, :, span], g_tile.at[spot, span]
        remote(source_piece, target, f_send, f_recv, (row_to, z, (1 - yl) * 2 + c))

        @pl.when(row_to != row)
        def _():
            remote(source_piece, target, f_own_send, f_recv, (row_to, z, dep))

        @pl.when(row_to == row)
        def _():
            g_tile[spot, span] = gz[s, :, span]

    def input_partial(s):
        w = w_pan[s // 4, s % 4]
        for t in range(2):
            term = lax.dot_general(
                og(s, t)[...], w, (((1,), (1,)), ((), ())), preferred_element_type=jnp.float32
            )
            if s == 0:
                acc[t] = term
            else:
                acc[t] += term

    def w_gather(parity, axis_peer, rows, n, send, recv):
        view = w_pan.at[parity, :, rows]
        for j in range(1, 4):
            remote(view, view, send, recv, axis_peer(j))

    def w_gathered(parity, n, recv):
        await_bytes(w_pan.at[parity, :, pl.ds(0, 3 * n)], recv)

    def pass_on(s, b, d):
        arrived(s, b, d)
        if s != 4:
            forward(s, b, d)
        to_sibling(s, b, d)

    rows_x = pl.ds(pl.multiple_of(x * 4 * U, 4 * U), 4 * U)
    rows_y = pl.ds(pl.multiple_of(y * 4 * U, 4 * U), 4 * U)

    forward(0, 1, 0)
    forward(0, 1, 1)
    await_bytes(og_all.at[0, 0], l_sem.at[2])
    await_bytes(ct_sib, m_recv.at[0])
    grad_partial(0, 0)
    grad_partial(0, 1)
    pass_on(7, 0, 0)
    pass_on(1, 0, 1)
    await_bytes(w_in.at[pl.ds(0, 7)], w_recv.at[1])
    w_gather(0, y_peer, pl.ds(place[0], U), U, w_send.at[2], w_recv.at[2])
    w_gather(1, x_peer, pl.ds(place[1], U), U, w_send.at[3], w_recv.at[3])
    grad_partial(7, 0)
    grad_partial(1, 0)
    pass_on(7, 1, 0)
    pass_on(1, 1, 1)
    w_gathered(0, U, w_recv.at[2])
    w_gather(0, x_peer, rows_x, 4 * U, w_send.at[4], w_recv.at[4])
    w_gathered(1, U, w_recv.at[3])
    w_gather(1, y_peer, rows_y, 4 * U, w_send.at[5], w_recv.at[5])
    grad_partial(7, 1)
    grad_partial(1, 1)
    reduce_first(0)
    pass_on(6, 0, 0)
    pass_on(2, 0, 1)
    grad_partial(6, 0)
    grad_partial(2, 0)
    pass_on(6, 1, 0)
    pass_on(2, 1, 1)
    reduce_first(7)
    reduce_first(1)
    grad_partial(6, 1)
    grad_partial(2, 1)
    pass_on(5, 0, 0)
    pass_on(3, 0, 1)
    reduce_second(0)
    reduce_second(7)
    reduce_second(1)
    grad_partial(5, 0)
    grad_partial(3, 0)
    reduce_first(6)
    reduce_first(2)
    deliver(0)
    pass_on(5, 1, 0)
    pass_on(3, 1, 1)
    grad_partial(5, 1)
    grad_partial(3, 1)
    reduce_second(6)
    reduce_second(2)
    w_gathered(0, 4 * U, w_recv.at[4])
    input_partial(0)
    pass_on(4, 0, 0)
    pass_on(4, 0, 1)
    input_partial(1)
    input_partial(2)
    grad_last(0)
    pass_on(4, 1, 0)
    pass_on(4, 1, 1)
    reduce_first(5)
    reduce_first(3)
    grad_last(1)
    w_gathered(1, 4 * U, w_recv.at[5])
    input_partial(7)
    input_partial(6)
    reduce_second(5)
    reduce_second(3)
    reduce_last(0)
    input_partial(5)
    input_partial(3)
    reduce_last(1)
    deliver(7)
    deliver(1)
    deliver(6)
    deliver(2)
    input_partial(4)
    ig_out[...] = acc[1].astype(jnp.bfloat16)
    remote(ig_out, ig_in, m_send.at[1], m_recv.at[1], sibling)
    deliver(5)
    deliver(3)
    deliver(4, 0)
    deliver(4, 1)
    ig_ref[:, ct_mine] = acc[0].astype(jnp.bfloat16)
    ct_other = pl.ds(pl.multiple_of(ct_half, half), half)

    await_bytes(g_tile.at[pl.ds(0, 15 * U)], f_recv)
    remote(g_tile, g_sib, m_send.at[2], m_recv.at[2], sibling)
    grad_ref[ct_mine, :] = g_tile[...]
    await_bytes(ig_in, m_recv.at[1])
    ig_ref[:, ct_other] = ig_in[...]
    await_bytes(g_sib, m_recv.at[2])
    grad_ref[ct_other, :] = g_sib[...]

    await_bytes(og_all.at[pl.ds(0, 7), 0], z_send)
    await_bytes(og_all.at[:, 1], s_send)
    await_bytes(ct_sib, m_send.at[0])
    await_bytes(ig_in, m_send.at[1])
    await_bytes(g_sib, m_send.at[2])
    await_bytes(w_in.at[pl.ds(0, 7)], w_send.at[0])
    await_bytes(w_in.at[pl.ds(0, 7)], w_send.at[1])
    w_gathered(0, U, w_send.at[2])
    w_gathered(1, U, w_send.at[3])
    w_gathered(0, 4 * U, w_send.at[4])
    w_gathered(1, 4 * U, w_send.at[5])
    for s in range(NZ):
        if s == 4:
            await_bytes(rd, r1_send.at[s])
        else:
            await_bytes(r1.at[s], r1_send.at[s])
            await_bytes(r2.at[s], r2_send.at[s])
    await_bytes(f_buf.at[pl.ds(0, 7)], h_send)
    await_bytes(gz, f_send)
    await_bytes(gz.at[pl.ds(0, 7)], f_own_send)


def update_kernel(
    input_ref,
    grad_ref,
    master_ref,
    first_ref,
    second_ref,
    input_out,
    master_out,
    first_out,
    second_out,
    master_v,
    first_v,
    second_v,
    input_sem,
    out_sem,
):
    copies = [pltpu.make_async_copy(input_ref, input_out, input_sem)]
    copies[0].start()
    n = grad_ref.shape[0] // PIECES
    for i in range(PIECES):
        rows = pl.ds(i * n, n)
        results = adam_update(
            grad_ref[rows, :].astype(jnp.float32),
            master_ref[rows, :],
            first_ref[rows, :],
            second_ref[rows, :],
        )
        held = (master_v, first_v, second_v)
        outs = (master_out, first_out, second_out)
        for k in range(3):
            held[k][rows, :] = results[k]
            copy = pltpu.make_async_copy(held[k].at[rows], outs[k].at[rows], out_sem.at[i, k])
            copy.start()
            copies.append(copy)
    for copy in copies:
        copy.wait()


def on_device(context, out_grad, master, first_moment, second_moment):
    tok, width = out_grad.shape
    bf16 = jnp.bfloat16
    half = 16 * U
    dma = pltpu.SemaphoreType.DMA
    vmem = pl.BlockSpec(memory_space=pltpu.VMEM)
    input_grad, gradient = pl.pallas_call(
        kernel,
        out_shape=(
            pltpu.VMEM((tok, 2 * half), bf16),
            pltpu.VMEM((2 * half, width), bf16),
        ),
        in_specs=[pl.BlockSpec(memory_space=pltpu.HBM)] * 3,
        out_specs=(vmem, vmem),
        scratch_shapes=[
            pltpu.VMEM((tok, 2 * half), bf16),
            pltpu.VMEM((2 * half, width), jnp.float32),
            pltpu.VMEM((NZ, 2, tok, width), bf16),
            pltpu.VMEM((2 * half, tok), bf16),
            pltpu.VMEM((half, tok), bf16),
            pltpu.VMEM((2 * half, width), bf16),
            pltpu.VMEM((8, U, width), bf16),
            pltpu.VMEM((2, NZ // 2, half, width), bf16),
            pltpu.VMEM((NZ, 4, 4 * U, width), bf16),
            pltpu.VMEM((NZ, 3, 4 * U, width), bf16),
            pltpu.VMEM((NZ, 4, U, width), bf16),
            pltpu.VMEM((NZ, 3, U, width), bf16),
            pltpu.VMEM((15, U, width), bf16),
            pltpu.VMEM((NZ, U, width), bf16),
            pltpu.VMEM((NZ, U, width), bf16),
            pltpu.VMEM((half, width), bf16),
            pltpu.VMEM((half, width), bf16),
            pltpu.VMEM((2, tok, half), jnp.float32),
            pltpu.VMEM((tok, half), bf16),
            pltpu.VMEM((tok, half), bf16),
            dma,
            dma((2, NZ, 2)),
            dma,
            dma((NZ, 2)),
            dma((3,)),
            dma((3,)),
            dma((6,)),
            dma((6,)),
            dma((NZ,)),
            dma((NZ,)),
            dma((NZ,)),
            dma((NZ,)),
            dma,
            dma((NZ,)),
            dma,
            dma,
            dma,
            dma((3,)),
            dma((2,)),
            dma((2,)),
        ],
        compiler_params=pltpu.CompilerParams(
            collective_id=0, has_side_effects=True, vmem_limit_bytes=56 * 1024 * 1024
        ),
        cost_estimate=pl.CostEstimate(
            flops=8 * tok * width * 2 * half * 2, bytes_accessed=4_000_000, transcendentals=0
        ),
    )(context, out_grad, master)
    hbm = pl.BlockSpec(memory_space=pltpu.HBM)
    tile = jax.ShapeDtypeStruct(master.shape, jnp.float32)
    return pl.pallas_call(
        update_kernel,
        out_shape=(jax.ShapeDtypeStruct(input_grad.shape, bf16), tile, tile, tile),
        in_specs=[vmem] * 5,
        out_specs=(hbm,) * 4,
        scratch_shapes=[
            pltpu.VMEM(master.shape, jnp.float32),
            pltpu.VMEM(master.shape, jnp.float32),
            pltpu.VMEM(master.shape, jnp.float32),
            dma,
            dma((PIECES, 3)),
        ],
        compiler_params=pltpu.CompilerParams(vmem_limit_bytes=8 * 1024 * 1024),
        cost_estimate=pl.CostEstimate(
            flops=20 * master.size, bytes_accessed=12 * master.size, transcendentals=2 * master.size
        ),
    )(input_grad, gradient, master, first_moment, second_moment)


def solution(mesh):
    in_specs = (
        P(("row", "depth"), "col"),
        P(("row", "depth"), "col"),
        P("row", "col"),
        P("row", "col"),
        P("row", "col"),
    )
    out_specs = (P(("row", "depth"), "col"), P("row", "col"), P("row", "col"), P("row", "col"))
    return jax.shard_map(
        on_device, mesh=mesh, in_specs=in_specs, out_specs=out_specs, check_vma=False
    )
```

```python
import jax
import jax.numpy as jnp
from jax import lax
from jax.experimental import pallas as pl
from jax.experimental.pallas import tpu as pltpu
from jax.sharding import PartitionSpec as P

STEP = 10

beta_one = 0.9
beta_two = 0.95
adam_eps = 1e-08
learn_rate = 0.001
decay_rate = 0.1

MESH = pl.DeviceIdType.MESH
NZ = 8
PIECES = 4
CUT = 256
U = 16


def adam_update(gradient, master, first_moment, second_moment):
    new_first = beta_one * first_moment + (1.0 - beta_one) * gradient
    new_second = beta_two * second_moment + (1.0 - beta_two) * gradient * gradient
    first_hat = new_first * (1.0 / (1.0 - beta_one**STEP))
    second_hat = new_second * (1.0 / (1.0 - beta_two**STEP))
    new_master = master - learn_rate * (
        first_hat / (jnp.sqrt(second_hat) + adam_eps) + decay_rate * master
    )
    return (new_master, new_first, new_second)


def mod(value, n):
    return lax.rem(value, jnp.int32(n))


def kernel(
    ctx_ref,
    og_ref,
    master_ref,
    ig_ref,
    grad_ref,
    ctx_v,
    master_v,
    og_all,
    ct_own,
    ct_sib,
    w16,
    w_in,
    w_pan,
    p_buf,
    r1,
    q_buf,
    r2,
    rd,
    f_buf,
    gz,
    g_tile,
    g_sib,
    acc,
    ig_out,
    ig_in,
    z_send,
    z_recv,
    s_send,
    s_recv,
    m_send,
    m_recv,
    w_send,
    w_recv,
    r1_send,
    r1_recv,
    r2_send,
    r2_recv,
    h_send,
    h_recv,
    f_send,
    f_own_send,
    f_recv,
    l_sem,
    d_recv,
    h_last_recv,
):
    row, z, dep = lax.axis_index("row"), lax.axis_index("col"), lax.axis_index("depth")
    x, yh = lax.div(row, jnp.int32(2)), mod(row, 2)
    yl, c = lax.div(dep, jnp.int32(2)), mod(dep, 2)
    y = yh * 2 + yl
    half = 16 * U
    tok = og_ref.shape[0]
    ht = tok // 2

    def z_peer(s):
        return (row, mod(z + s, NZ), dep)

    sibling = (row, z, yl * 2 + (1 - c))

    def x_peer(j):
        return (mod(x + j, 4) * 2 + yh, z, dep)

    def y_peer(j):
        yy = mod(y + j, 4)
        return (x * 2 + lax.div(yy, jnp.int32(2)), z, mod(yy, 2) * 2 + c)

    def remote(src, dst, send, recv, device):
        pltpu.make_async_remote_copy(
            src_ref=src,
            dst_ref=dst,
            send_sem=send,
            recv_sem=recv,
            device_id=device,
            device_id_type=MESH,
        ).start()

    def await_bytes(ref, sem):
        pltpu.make_async_copy(ref, ref, sem).wait()

    place = (
        pl.multiple_of(x * (4 * U) + y * U, U),
        pl.multiple_of(y * (4 * U) + x * U, U),
    )

    pltpu.make_async_copy(master_ref, master_v, l_sem.at[0]).start()
    pltpu.make_async_copy(ctx_ref, ctx_v, l_sem.at[1]).start()
    pltpu.make_async_copy(og_ref, og_all.at[0, 0], l_sem.at[2]).start()
    barrier = pltpu.get_barrier_semaphore()
    for s in range(1, NZ):
        pl.semaphore_signal(barrier, inc=1, device_id=z_peer(s), device_id_type=MESH)
    pl.semaphore_signal(barrier, inc=1, device_id=sibling, device_id_type=MESH)
    for j in range(8):
        for e in range(2):
            if j or e:
                pl.semaphore_signal(
                    barrier,
                    inc=1,
                    device_id=(mod(row + j, 8), z, mod(yl + e, 2) * 2 + c),
                    device_id_type=MESH,
                )
    pl.semaphore_wait(barrier, 23)

    def og(s, t):
        return og_all.at[s, t]

    def source(s):
        return og_ref if s == 0 else og_all.at[s, 0]

    cols = (pl.ds(0, CUT), pl.ds(CUT, og_ref.shape[1] - CUT))

    def part(ref, b, d=None):
        return ref.at[:, cols[b]] if d is None else ref.at[pl.ds(d * ht, ht), cols[b]]

    def token_half(s, d):
        return d if s == 4 else None

    def forward(s, b, d):
        to, peer = ((s - 1) % NZ, z_peer(1)) if d == 0 else (s + 1, z_peer(NZ - 1))
        h = token_half(to, d)
        remote(
            part(source(s), b, h),
            part(og_all.at[to, 0], b, h),
            z_send,
            z_recv.at[d, to, b],
            peer,
        )

    def to_sibling(s, b, d=0):
        h = token_half(s, d)
        remote(
            part(source(s), b, h), part(og_all.at[s, 1], b, h), s_send, s_recv.at[s, b], sibling
        )

    def arrived(s, b, d):
        await_bytes(part(og_all.at[s, 0], b, token_half(s, d)), z_recv.at[d, s, b])

    forward(0, 0, 0)
    forward(0, 0, 1)
    await_bytes(master_v, l_sem.at[0])
    w16[...] = master_v[...].astype(jnp.bfloat16)

    late = lax.div(mod(z + NZ - row, NZ), jnp.int32(4))

    def w_place(row_to):
        xx, yy = lax.div(row_to, jnp.int32(2)), mod(row_to, 2) * 2 + yl
        a, b = xx + late * (yy - xx), yy + late * (xx - yy)
        return pl.ds(pl.multiple_of(c * half + a * (4 * U) + b * U, U), U)

    for j in range(1, 8):
        row_to = mod(row + j, 8)
        remote(
            w16.at[w_place(row_to)], w_in.at[row], w_send.at[0], w_recv.at[0], (row_to, z, dep)
        )
    w_in[row] = w16[w_place(row)]
    await_bytes(ctx_v, l_sem.at[1])
    ct_own[...] = ctx_v[...].T
    ct_half = (1 - c) * half
    remote(
        ct_own.at[pl.ds(pl.multiple_of(ct_half, half), half)],
        ct_sib,
        m_send.at[0],
        m_recv.at[0],
        sibling,
    )

    to_sibling(0, 0)
    to_sibling(0, 1)

    await_bytes(w_in.at[pl.ds(0, 7)], w_recv.at[0])

    for step in range(1, NZ):
        s = NZ - step
        remote(
            w_in.at[mod(z + step, NZ)],
            w_pan.at[s // 4, s % 4, pl.ds(place[s // 4], U)],
            w_send.at[1],
            w_recv.at[1],
            z_peer(step),
        )
    w_pan[0, 0, pl.ds(place[0], U)] = w_in[z]

    ct_mine = pl.ds(pl.multiple_of(c * half, half), half)

    def grad_terms(s, b):
        await_bytes(part(og_all.at[s, 1], b), s_recv.at[s, b])
        total = jnp.dot(
            ct_own[ct_mine, :], og_all[s, 0, :, cols[b]], preferred_element_type=jnp.float32
        )
        total += jnp.dot(
            ct_sib[...], og_all[s, 1, :, cols[b]], preferred_element_type=jnp.float32
        )
        p_buf[s, :, :, cols[b]] = total.astype(jnp.bfloat16).reshape(4, 4 * U, total.shape[-1])

    def grad_partial(s, b):
        grad_terms(s, b)
        axis, peer = (x, x_peer) if s < 4 else (y, y_peer)
        for j in range(1, 4):
            remote(
                p_buf.at[s, mod(axis + j, 4), :, cols[b]],
                r1.at[s, j - 1, :, cols[b]],
                r1_send.at[s],
                r1_recv.at[s],
                peer(j),
            )

    def reduce_first(s):
        await_bytes(r1.at[s], r1_recv.at[s])
        axis = x if s < 4 else y
        total = p_buf[s, axis].astype(jnp.float32)
        for j in range(3):
            total += r1[s, j].astype(jnp.float32)
        q_buf[s] = total.astype(jnp.bfloat16).reshape(4, U, total.shape[-1])
        axis, peer = (y, y_peer) if s < 4 else (x, x_peer)
        for j in range(1, 4):
            remote(
                q_buf.at[s, mod(axis + j, 4)],
                r2.at[s, j - 1],
                r2_send.at[s],
                r2_recv.at[s],
                peer(j),
            )

    def reduce_second(s):
        await_bytes(r2.at[s], r2_recv.at[s])
        axis = y if s < 4 else x
        total = q_buf[s, axis].astype(jnp.float32)
        for j in range(3):
            total += r2[s, j].astype(jnp.float32)
        if s == 0:
            gz[0] = total.astype(jnp.bfloat16)
        else:
            f_buf[s] = total.astype(jnp.bfloat16)
            remote(f_buf.at[s], gz.at[s], h_send, h_recv.at[s], z_peer(s))

    def grad_last(b):
        grad_terms(4, b)
        for jx in (2, 1, 3, 0):
            for jy in (2, 1, 3, 0):
                if jx or jy:
                    xx, yy = mod(x + jx, 4), mod(y + jy, 4)
                    remote(
                        p_buf.at[4, yy, pl.ds(pl.multiple_of(xx * U, U), U), cols[b]],
                        rd.at[jx * 4 + jy - 1, :, cols[b]],
                        r1_send.at[4],
                        d_recv.at[b],
                        (xx * 2 + lax.div(yy, jnp.int32(2)), z, mod(yy, 2) * 2 + c),
                    )

    def reduce_last(b):
        await_bytes(rd.at[:, :, cols[b]], d_recv.at[b])
        total = p_buf[4, y, pl.ds(pl.multiple_of(x * U, U), U), cols[b]].astype(jnp.float32)
        for j in range(15):
            total += rd[j, :, cols[b]].astype(jnp.float32)
        f_buf[4, :, cols[b]] = total.astype(jnp.bfloat16)
        remote(
            f_buf.at[4, :, cols[b]], gz.at[4, :, cols[b]], h_send, h_last_recv.at[b], z_peer(4)
        )

    def deliver(s, b=None):
        span = slice(None) if b is None else cols[b]
        if s == 4:
            await_bytes(gz.at[4, :, span], h_last_recv.at[b])
        elif s:
            await_bytes(gz.at[s], h_recv.at[s])
        row_to = mod(z + (NZ - s), NZ)
        spot = pl.ds(place[s // 4], U)
        source_piece, target = gz.at[s, :, span], g_tile.at[spot, span]
        remote(source_piece, target, f_send, f_recv, (row_to, z, (1 - yl) * 2 + c))

        @pl.when(row_to != row)
        def _():
            remote(source_piece, target, f_own_send, f_recv, (row_to, z, dep))

        @pl.when(row_to == row)
        def _():
            g_tile[spot, span] = gz[s, :, span]

    def input_partial(s):
        w = w_pan[s // 4, s % 4]
        for t in range(2):
            term = lax.dot_general(
                og(s, t)[...], w, (((1,), (1,)), ((), ())), preferred_element_type=jnp.float32
            )
            if s == 0:
                acc[t] = term
            else:
                acc[t] += term

    def w_gather(parity, axis_peer, rows, n, send, recv):
        view = w_pan.at[parity, :, rows]
        for j in range(1, 4):
            remote(view, view, send, recv, axis_peer(j))

    def w_gathered(parity, n, recv):
        await_bytes(w_pan.at[parity, :, pl.ds(0, 3 * n)], recv)

    def pass_on(s, b, d):
        arrived(s, b, d)
        if s != 4:
            forward(s, b, d)
        to_sibling(s, b, d)

    rows_x = pl.ds(pl.multiple_of(x * 4 * U, 4 * U), 4 * U)
    rows_y = pl.ds(pl.multiple_of(y * 4 * U, 4 * U), 4 * U)

    forward(0, 1, 0)
    forward(0, 1, 1)
    await_bytes(og_all.at[0, 0], l_sem.at[2])
    await_bytes(ct_sib, m_recv.at[0])
    grad_partial(0, 0)
    grad_partial(0, 1)
    pass_on(7, 0, 0)
    pass_on(1, 0, 1)
    await_bytes(w_in.at[pl.ds(0, 7)], w_recv.at[1])
    w_gather(0, y_peer, pl.ds(place[0], U), U, w_send.at[2], w_recv.at[2])
    w_gather(1, x_peer, pl.ds(place[1], U), U, w_send.at[3], w_recv.at[3])
    grad_partial(7, 0)
    grad_partial(1, 0)
    pass_on(7, 1, 0)
    pass_on(1, 1, 1)
    w_gathered(0, U, w_recv.at[2])
    w_gather(0, x_peer, rows_x, 4 * U, w_send.at[4], w_recv.at[4])
    w_gathered(1, U, w_recv.at[3])
    w_gather(1, y_peer, rows_y, 4 * U, w_send.at[5], w_recv.at[5])
    grad_partial(7, 1)
    grad_partial(1, 1)
    reduce_first(0)
    pass_on(6, 0, 0)
    pass_on(2, 0, 1)
    grad_partial(6, 0)
    grad_partial(2, 0)
    pass_on(6, 1, 0)
    pass_on(2, 1, 1)
    grad_partial(6, 1)
    grad_partial(2, 1)
    reduce_first(7)
    reduce_first(1)
    pass_on(5, 0, 0)
    pass_on(3, 0, 1)
    reduce_second(0)
    reduce_second(7)
    reduce_second(1)
    grad_partial(5, 0)
    grad_partial(3, 0)
    reduce_first(6)
    reduce_first(2)
    deliver(0)
    pass_on(5, 1, 0)
    pass_on(3, 1, 1)
    grad_partial(5, 1)
    grad_partial(3, 1)
    reduce_second(6)
    reduce_second(2)
    w_gathered(0, 4 * U, w_recv.at[4])
    input_partial(0)
    pass_on(4, 0, 0)
    pass_on(4, 0, 1)
    input_partial(1)
    input_partial(2)
    grad_last(0)
    pass_on(4, 1, 0)
    pass_on(4, 1, 1)
    reduce_first(5)
    reduce_first(3)
    grad_last(1)
    w_gathered(1, 4 * U, w_recv.at[5])
    input_partial(7)
    input_partial(6)
    reduce_second(5)
    reduce_second(3)
    reduce_last(0)
    input_partial(5)
    input_partial(3)
    reduce_last(1)
    deliver(7)
    deliver(1)
    deliver(6)
    deliver(2)
    input_partial(4)
    ig_out[...] = acc[1].astype(jnp.bfloat16)
    remote(ig_out, ig_in, m_send.at[1], m_recv.at[1], sibling)
    deliver(5)
    deliver(3)
    deliver(4, 0)
    deliver(4, 1)
    ig_ref[:, ct_mine] = acc[0].astype(jnp.bfloat16)
    ct_other = pl.ds(pl.multiple_of(ct_half, half), half)

    await_bytes(g_tile.at[pl.ds(0, 15 * U)], f_recv)
    remote(g_tile, g_sib, m_send.at[2], m_recv.at[2], sibling)
    grad_ref[ct_mine, :] = g_tile[...]
    await_bytes(ig_in, m_recv.at[1])
    ig_ref[:, ct_other] = ig_in[...]
    await_bytes(g_sib, m_recv.at[2])
    grad_ref[ct_other, :] = g_sib[...]

    await_bytes(og_all.at[pl.ds(0, 7), 0], z_send)
    await_bytes(og_all.at[:, 1], s_send)
    await_bytes(ct_sib, m_send.at[0])
    await_bytes(ig_in, m_send.at[1])
    await_bytes(g_sib, m_send.at[2])
    await_bytes(w_in.at[pl.ds(0, 7)], w_send.at[0])
    await_bytes(w_in.at[pl.ds(0, 7)], w_send.at[1])
    w_gathered(0, U, w_send.at[2])
    w_gathered(1, U, w_send.at[3])
    w_gathered(0, 4 * U, w_send.at[4])
    w_gathered(1, 4 * U, w_send.at[5])
    for s in range(NZ):
        if s == 4:
            await_bytes(rd, r1_send.at[s])
        else:
            await_bytes(r1.at[s], r1_send.at[s])
            await_bytes(r2.at[s], r2_send.at[s])
    await_bytes(f_buf.at[pl.ds(0, 7)], h_send)
    await_bytes(gz, f_send)
    await_bytes(gz.at[pl.ds(0, 7)], f_own_send)


def update_kernel(
    input_ref,
    grad_ref,
    master_ref,
    first_ref,
    second_ref,
    input_out,
    master_out,
    first_out,
    second_out,
    master_v,
    first_v,
    second_v,
    input_sem,
    out_sem,
):
    copies = [pltpu.make_async_copy(input_ref, input_out, input_sem)]
    copies[0].start()
    n = grad_ref.shape[0] // PIECES
    for i in range(PIECES):
        rows = pl.ds(i * n, n)
        results = adam_update(
            grad_ref[rows, :].astype(jnp.float32),
            master_ref[rows, :],
            first_ref[rows, :],
            second_ref[rows, :],
        )
        held = (master_v, first_v, second_v)
        outs = (master_out, first_out, second_out)
        for k in range(3):
            held[k][rows, :] = results[k]
            copy = pltpu.make_async_copy(held[k].at[rows], outs[k].at[rows], out_sem.at[i, k])
            copy.start()
            copies.append(copy)
    for copy in copies:
        copy.wait()


def on_device(context, out_grad, master, first_moment, second_moment):
    tok, width = out_grad.shape
    bf16 = jnp.bfloat16
    half = 16 * U
    dma = pltpu.SemaphoreType.DMA
    vmem = pl.BlockSpec(memory_space=pltpu.VMEM)
    input_grad, gradient = pl.pallas_call(
        kernel,
        out_shape=(
            pltpu.VMEM((tok, 2 * half), bf16),
            pltpu.VMEM((2 * half, width), bf16),
        ),
        in_specs=[pl.BlockSpec(memory_space=pltpu.HBM)] * 3,
        out_specs=(vmem, vmem),
        scratch_shapes=[
            pltpu.VMEM((tok, 2 * half), bf16),
            pltpu.VMEM((2 * half, width), jnp.float32),
            pltpu.VMEM((NZ, 2, tok, width), bf16),
            pltpu.VMEM((2 * half, tok), bf16),
            pltpu.VMEM((half, tok), bf16),
            pltpu.VMEM((2 * half, width), bf16),
            pltpu.VMEM((8, U, width), bf16),
            pltpu.VMEM((2, NZ // 2, half, width), bf16),
            pltpu.VMEM((NZ, 4, 4 * U, width), bf16),
            pltpu.VMEM((NZ, 3, 4 * U, width), bf16),
            pltpu.VMEM((NZ, 4, U, width), bf16),
            pltpu.VMEM((NZ, 3, U, width), bf16),
            pltpu.VMEM((15, U, width), bf16),
            pltpu.VMEM((NZ, U, width), bf16),
            pltpu.VMEM((NZ, U, width), bf16),
            pltpu.VMEM((half, width), bf16),
            pltpu.VMEM((half, width), bf16),
            pltpu.VMEM((2, tok, half), jnp.float32),
            pltpu.VMEM((tok, half), bf16),
            pltpu.VMEM((tok, half), bf16),
            dma,
            dma((2, NZ, 2)),
            dma,
            dma((NZ, 2)),
            dma((3,)),
            dma((3,)),
            dma((6,)),
            dma((6,)),
            dma((NZ,)),
            dma((NZ,)),
            dma((NZ,)),
            dma((NZ,)),
            dma,
            dma((NZ,)),
            dma,
            dma,
            dma,
            dma((3,)),
            dma((2,)),
            dma((2,)),
        ],
        compiler_params=pltpu.CompilerParams(
            collective_id=0, has_side_effects=True, vmem_limit_bytes=56 * 1024 * 1024
        ),
        cost_estimate=pl.CostEstimate(
            flops=8 * tok * width * 2 * half * 2, bytes_accessed=4_000_000, transcendentals=0
        ),
    )(context, out_grad, master)
    hbm = pl.BlockSpec(memory_space=pltpu.HBM)
    tile = jax.ShapeDtypeStruct(master.shape, jnp.float32)
    return pl.pallas_call(
        update_kernel,
        out_shape=(jax.ShapeDtypeStruct(input_grad.shape, bf16), tile, tile, tile),
        in_specs=[vmem] * 5,
        out_specs=(hbm,) * 4,
        scratch_shapes=[
            pltpu.VMEM(master.shape, jnp.float32),
            pltpu.VMEM(master.shape, jnp.float32),
            pltpu.VMEM(master.shape, jnp.float32),
            dma,
            dma((PIECES, 3)),
        ],
        compiler_params=pltpu.CompilerParams(vmem_limit_bytes=8 * 1024 * 1024),
        cost_estimate=pl.CostEstimate(
            flops=20 * master.size, bytes_accessed=12 * master.size, transcendentals=2 * master.size
        ),
    )(input_grad, gradient, master, first_moment, second_moment)


def solution(mesh):
    in_specs = (
        P(("row", "depth"), "col"),
        P(("row", "depth"), "col"),
        P("row", "col"),
        P("row", "col"),
        P("row", "col"),
    )
    out_specs = (P(("row", "depth"), "col"), P("row", "col"), P("row", "col"), P("row", "col"))
    return jax.shard_map(
        on_device, mesh=mesh, in_specs=in_specs, out_specs=out_specs, check_vma=False
    )
```
